32 devices in a mesh: dp: 8 (over z, x), mp: 4 (over y, core).
Axes of the slice: x: 2, y: 2, z: 4, core: 2. Of those that a mesh axis runs over, the one named last changes fastest.
Arguments:
- captions: bfloat16 [4096, 768], P(('dp', 'mp')), may hold values from -6 to 6
- features: bfloat16 [4096, 2048], P(('dp', 'mp')), may hold values from -6 to 6
- region_boxes: float32 [4, 4096], P(None, ('dp', 'mp')), may hold values from 0 to 1
- caption_counts: int32 [32], P('dp'), may hold values from 8 to 128
- region_counts: int32 [32], P('dp'), may hold values from 36 to 100
- slot_map: int32 [32, 128], P(('dp', 'mp')), may hold values from 0 to 127, each once within a row
- w_feat: bfloat16 [2048, 768], replicated, may hold values from -0.125 to 0.125
- w_box: float32 [4, 768], replicated, may hold values from -3 to 3
- enc_gain: float32 [768], replicated, may hold values from 0.25 to 1.75
- enc_vectors: float32 [2, 768], replicated, may hold values from -3 to 3
- w_qkv: bfloat16 [2, 768, 3, 768], P(None, None, None, 'mp'), may hold values from -0.21875 to 0.21875
- b_qv: float32 [2, 2, 768], P(None, None, 'mp'), may hold values from -3 to 3
- w_out: bfloat16 [2, 768, 768], P(None, 'mp'), may hold values from -0.875 to 0.875
- w_up: bfloat16 [2, 768, 3072], P(None, None, 'mp'), may hold values from -0.21875 to 0.21875
- b_up: float32 [2, 3072], P(None, 'mp'), may hold values from -3 to 3
- w_down: bfloat16 [2, 3072, 768], P(None, 'mp'), may hold values from -0.109375 to 0.109375
- norm_gains: float32 [2, 2, 768], replicated, may hold values from 0.25 to 1.75
- row_biases: float32 [2, 4, 768], replicated, may hold values from -3 to 3
- cotangent: bfloat16 [8192, 768], P(('dp', 'mp')), may hold values from -6 to 6
Outputs:
- layer_output: float32 [8192, 768], P(('dp', 'mp'))
- caption_grad: float32 [4096, 768], P(('dp', 'mp'))
- feature_grad: float32 [4096, 2048], P(('dp', 'mp'))
- w_feat_grad: float32 [2048, 768], replicated
- w_box_grad: float32 [4, 768], replicated
- enc_gain_grad: float32 [768], replicated
- enc_vectors_grad: float32 [2, 768], replicated
- w_qkv_grad: float32 [2, 768, 3, 768], P(None, None, None, 'mp')
- b_qv_grad: float32 [2, 2, 768], P(None, None, 'mp')
- w_out_grad: float32 [2, 768, 768], P(None, 'mp')
- w_up_grad: float32 [2, 768, 3072], P(None, None, 'mp')
- b_up_grad: float32 [2, 3072], P(None, 'mp')
- w_down_grad: float32 [2, 3072, 768], P(None, 'mp')
- norm_gains_grad: float32 [2, 2, 768], replicated
- row_biases_grad: float32 [2, 4, 768], replicated
The draws below stay inside these ranges and needn't reach their ends.
Inputs may be any that keep to these rules, and one draw needn't show every extreme that they name: Each row of slot_map is a permutation of 0 to 127.
All inputs are finite; a program needn't handle non-finite values.
Results may differ from the reference program's by a relative error of at most 0.025.
Values may be sent and summed in bfloat16 or wider, within the bound.
A program may use at most 128 MiB of HBM per device.

```python
import jax
import jax.numpy as jnp
from jax import lax

D = 768
HEADS = 12
HD = 64
FF = 3072
FEAT = 2048
CAP = 128
RPAD = 128
RMAX = 100
LAYERS = 2
IMG_DEV = 1
SEQ = 256
IMAGES = 32
N_DP = 8
N_MP = 4


def plant(result, own_key, least, high):
    spot = [jax.random.randint(jax.random.fold_in(own_key, axis), (), 0, length) for axis, length in enumerate(result.shape)]
    widest = result.shape.index(max(result.shape))
    next_to = spot[:widest] + [(spot[widest] + 1) % result.shape[widest]] + spot[widest + 1:]
    return result.at[tuple(spot)].set(least).at[tuple(next_to)].set(high)


def levels(own_key, shape, cuts, smallest, largest):
    def one(dim, blocks):
        steps = jax.random.uniform(jax.random.fold_in(jax.random.fold_in(own_key, 6), dim), (blocks,), jnp.float32, smallest / len(cuts), largest / len(cuts))
        return jnp.repeat(jnp.exp(steps), shape[dim] // blocks).reshape((-1,) + (1,) * (len(shape) - dim - 1))

    level = one(*cuts[0])
    for cut in cuts[1:]:
        level = level * one(*cut)
    return level


def scatter_about(rng, extent, scale, most, split=(), kind=jnp.bfloat16):
    entries = scale * jax.random.normal(rng, extent, jnp.float32)
    if split:
        entries = entries * levels(rng, extent, split, -0.22, 0.18)
    return jnp.clip(entries, -most, most).astype(kind)


def setup_inputs(seed: int = 0) -> dict:
    keys = jax.random.split(jax.random.key(seed), 20)
    captions = scatter_about(keys[0], (IMAGES * CAP, D), 1.0, 6.0, ((0, 32),))
    features = scatter_about(keys[1], (IMAGES * RPAD, FEAT), 1.0, 6.0, ((0, 32),))
    region_boxes = jnp.clip(1.0 * jax.random.uniform(keys[2], (4, IMAGES * RPAD), jnp.float32) ** levels(keys[2], (4, IMAGES * RPAD), ((1, 32),), -0.2, 0.2), 0.0, 1.0)
    caption_counts = plant(jax.random.randint(keys[3], (IMAGES,), max(1, CAP // 16), CAP + 1), jax.random.fold_in(keys[3], 1), max(1, CAP // 16), CAP).astype(jnp.int32)
    region_counts = plant(jax.random.randint(keys[4], (IMAGES,), RMAX * 9 // 25, RMAX + 1), jax.random.fold_in(keys[4], 1), RMAX * 9 // 25, RMAX).astype(jnp.int32)
    slot_map = jax.vmap(lambda own: jax.random.permutation(own, IMG_DEV * RPAD))(jax.random.split(keys[5], (N_DP * N_MP))).reshape((N_DP * N_MP, IMG_DEV * RPAD)).astype(jnp.int32)
    w_feat = scatter_about(keys[6], (FEAT, D), FEAT ** -0.5, 0.125)
    w_box = scatter_about(keys[7], (4, D), 4 ** -0.5, 3.0, (), jnp.float32)
    enc_gain = jnp.clip(1.0 + 0.15 * jax.random.normal(keys[8], (D,), jnp.float32), 0.25, 1.75)
    enc_vectors = scatter_about(keys[9], (2, D), 0.5, 3.0, (), jnp.float32)
    w_qkv = scatter_about(keys[10], (LAYERS, D, 3, D), D ** -0.5, 0.21875, ((3, 4),))
    b_qv = scatter_about(keys[11], (LAYERS, 2, D), 0.5, 3.0, ((2, 4),), jnp.float32)
    w_out = scatter_about(keys[12], (LAYERS, D, D), (D // 16) ** -0.5, 0.875, ((1, 4),))
    w_up = scatter_about(keys[13], (LAYERS, D, FF), D ** -0.5, 0.21875, ((2, 4),))
    b_up = scatter_about(keys[14], (LAYERS, FF), 0.5, 3.0, ((1, 4),), jnp.float32)
    w_down = scatter_about(keys[15], (LAYERS, FF, D), FF ** -0.5, 0.109375, ((1, 4),))
    norm_gains = jnp.clip(1.0 + 0.15 * jax.random.normal(keys[16], (LAYERS, 2, D), jnp.float32), 0.25, 1.75)
    row_biases = scatter_about(keys[17], (LAYERS, 4, D), 0.5, 3.0, (), jnp.float32)
    cotangent = scatter_about(keys[18], (IMAGES * SEQ, D), 1.0, 6.0, ((0, 32),))
    return dict(captions=captions, features=features, region_boxes=region_boxes, caption_counts=caption_counts, region_counts=region_counts, slot_map=slot_map, w_feat=w_feat, w_box=w_box, enc_gain=enc_gain, enc_vectors=enc_vectors, w_qkv=w_qkv, b_qv=b_qv, w_out=w_out, w_up=w_up, b_up=b_up, w_down=w_down, norm_gains=norm_gains, row_biases=row_biases, cotangent=cotangent)


@jax.custom_vjp
def low(v):
    return lax.optimization_barrier(v.astype(jnp.bfloat16)).astype(jnp.float32)

@jax.custom_vjp
def low_back(v):
    return v

def low_keep(v):
    return (low(v), None)

def low_pass(kept, grad):
    return (grad,)

def back_keep(v):
    return (v, None)

def back_low(kept, grad):
    return (low(grad),)
low.defvjp(low_keep, low_pass)
low_back.defvjp(back_keep, back_low)
highest = lax.Precision.HIGHEST
epsilon = 1e-05
image_block = 16

def layer_norm(values, gain_vec, bias_vec):
    centre = values - lax.optimization_barrier(jnp.mean(values, axis=-1, keepdims=True))
    spread = lax.optimization_barrier(jnp.mean(centre * centre, axis=-1, keepdims=True))
    return centre * lax.rsqrt(spread + epsilon) * gain_vec + bias_vec

def attend(one_block):
    queries, keys_in, values_in, visible = one_block
    scores = jnp.einsum('bqhe,bkhe->bhqk', queries, keys_in, precision=highest) * HD ** (-0.5)
    scores = low_back(scores)
    scores = jnp.where(visible[:, None, None, :], scores, -1e+30)
    weights = low(jax.nn.softmax(scores, axis=-1))
    return jnp.einsum('bhqk,bkhe->bqhe', weights, values_in, precision=highest)

def block_layer(states, depth, visible, w_qkv, b_qv, w_out, w_up, b_up, w_down, norm_gains, row_biases):
    lowered = low(states)
    mixed_qkv = jnp.einsum('rd,dcf->rcf', lowered, w_qkv[depth], precision=highest)
    queries = low_back(low(mixed_qkv[:, 0] + b_qv[depth, 0]))
    keys_in = low_back(low(mixed_qkv[:, 1]))
    values_in = low_back(low(mixed_qkv[:, 2] + b_qv[depth, 1]))
    blocks = IMAGES // image_block
    head_shape = (blocks, image_block, SEQ, HEADS, HD)
    context = lax.map(jax.checkpoint(attend), (queries.reshape(head_shape), keys_in.reshape(head_shape), values_in.reshape(head_shape), visible.reshape(blocks, image_block, SEQ)))
    context = low_back(low(context.reshape(-1, D)))
    attn_out = low_back(jnp.dot(context, w_out[depth], precision=highest))
    pre_attn = states + attn_out + row_biases[depth, 0]
    normed = layer_norm(pre_attn, norm_gains[depth, 0], row_biases[depth, 1])
    up_pre = low_back(jnp.dot(low(normed), w_up[depth], precision=highest) + b_up[depth])
    activated = low(jax.nn.gelu(up_pre, approximate=False))
    ffn_out = low_back(jnp.dot(activated, w_down[depth], precision=highest))
    pre_ffn = normed + ffn_out + row_biases[depth, 2]
    return layer_norm(pre_ffn, norm_gains[depth, 1], row_biases[depth, 3])

def place_rows(got_rows, got_map):
    return jnp.zeros_like(got_rows).at[got_map].set(got_rows)

def reference(captions, features, region_boxes, caption_counts, region_counts, slot_map, w_feat, w_box, enc_gain, enc_vectors, w_qkv, b_qv, w_out, w_up, b_up, w_down, norm_gains, row_biases, cotangent):
    positions = jnp.arange(SEQ)[None, :]
    visible = jnp.where(positions < CAP, positions < caption_counts[:, None], positions - CAP < region_counts[:, None])

    def forward(captions_in, features_in, w_feat_in, w_box_in, enc_gain_in, enc_vectors_in, w_qkv_in, b_qv_in, w_out_in, w_up_in, b_up_in, w_down_in, norm_gains_in, row_biases_in):
        enc_pre = jnp.dot(features_in, w_feat_in, precision=highest)
        enc_pre = enc_pre + jnp.einsum('cr,cd->rd', region_boxes, w_box_in, precision=highest) + enc_vectors_in[0]
        enc_pre = low_back(enc_pre)
        encoded = low_back(low(layer_norm(enc_pre, enc_gain_in, enc_vectors_in[1])))
        peer_rows = IMG_DEV * RPAD // N_DP
        received = encoded.reshape(N_DP, N_MP, N_DP, peer_rows, D).transpose(2, 1, 0, 3, 4)
        received = received.reshape(N_DP * N_MP, IMG_DEV * RPAD, D)
        slot_rows = jax.vmap(place_rows)(received, slot_map)
        states = jnp.concatenate([captions_in.reshape(IMAGES, CAP, D), slot_rows.reshape(IMAGES, RPAD, D)], axis=1)
        states = states.reshape(IMAGES * SEQ, D)
        for depth in range(LAYERS):
            states = block_layer(states, depth, visible, w_qkv_in, b_qv_in, w_out_in, w_up_in, b_up_in, w_down_in, norm_gains_in, row_biases_in)
        return states
    primals = (captions.astype(jnp.float32), features.astype(jnp.float32), w_feat.astype(jnp.float32), w_box, enc_gain, enc_vectors, w_qkv.astype(jnp.float32), b_qv, w_out.astype(jnp.float32), w_up.astype(jnp.float32), b_up, w_down.astype(jnp.float32), norm_gains, row_biases)
    output, pullback = jax.vjp(forward, *primals)
    gradient = pullback(cotangent.astype(jnp.float32))
    return (output, gradient[0], gradient[1], gradient[2], gradient[3], gradient[4], gradient[5], gradient[6], gradient[7], gradient[8], gradient[9], gradient[10], gradient[11], gradient[12], gradient[13])
```

```python
import functools

import jax
import jax.numpy as jnp
from jax import lax
from jax.experimental import pallas as pl
from jax.experimental.pallas import tpu as pltpu
from jax.sharding import PartitionSpec as P

HD = 64
CAP = 128
RPAD = 128
LAYERS = 2
SEQ = 256
ROWS = SEQ
HALF = ROWS // 2
LANES = 256
GROUP = 4
COPIES = 10
LOW, FULL = jnp.bfloat16, jnp.float32
MESH = pl.DeviceIdType.MESH

epsilon = 1e-05


def dot_nn(left, right):
    return jnp.dot(left, right, preferred_element_type=FULL)


def dot_nt(left, right):
    return lax.dot_general(left, right, (((1,), (1,)), ((), ())), preferred_element_type=FULL)


def dot_tn(left, right):
    return lax.dot_general(left, right, (((0,), (0,)), ((), ())), preferred_element_type=FULL)


def row_sum(values):
    return jnp.sum(values, axis=0, keepdims=True)


def normed_rows(values):
    centre = values - jnp.mean(values, axis=-1, keepdims=True)
    spread = jnp.mean(centre * centre, axis=-1, keepdims=True)
    inverse = lax.rsqrt(spread + epsilon)
    return centre * inverse, inverse


def normed_back(gradient, values, gain):
    hat, inverse = normed_rows(values)
    scaled = gradient * gain
    tilt = jnp.mean(scaled * hat, axis=-1, keepdims=True)
    level = jnp.mean(scaled, axis=-1, keepdims=True)
    return inverse * (scaled - level - hat * tilt), hat


def head_masks():
    lane = lax.broadcasted_iota(jnp.int32, (1, LANES), 1)
    return [
        jnp.where((lane >= head * HD) & (lane < head * HD + HD), 1.0, 0.0).astype(LOW)
        for head in range(3)
    ]


def image_rows(image):
    return pl.ds(pl.multiple_of(image * ROWS, ROWS), ROWS)


def half_rows(half, image=0):
    return pl.ds(pl.multiple_of(image * ROWS + half * HALF, HALF), HALF)


def remote(src, dst, send_sem, recv_sem, target):
    return pltpu.make_async_remote_copy(
        src_ref=src,
        dst_ref=dst,
        send_sem=send_sem,
        recv_sem=recv_sem,
        device_id=target,
        device_id_type=MESH,
    )


def greet(targets):
    barrier = pltpu.get_barrier_semaphore()
    for target in targets:
        pl.semaphore_signal(barrier, inc=1, device_id=target, device_id_type=MESH)
    pl.semaphore_wait(barrier, len(targets))


class Loads:
    def __init__(self, sems):
        self.sems, self.used, self.made = sems, 0, []

    def start(self, src, dst):
        one = pltpu.make_async_copy(src, dst, self.sems.at[self.used])
        self.used += 1
        self.made.append(one)
        one.start()
        return one


class Group:
    def __init__(self, scratch):
        self.me = lax.axis_index("mp")
        self.core = lax.rem(self.me, 2)
        self.mate = self.me + 1 - 2 * self.core
        self.peer = lax.rem(self.me + 2, GROUP)
        self.diag = lax.rem(self.mate + 2, GROUP)
        self.near = self.me - self.core
        self.far = self.peer - self.core
        (
            self.acc, self.far_acc, self.near_sums, self.mixed_sums, self.far_sums, self.out_sums,
            self.send, self.recv,
        ) = scratch

    def others(self):
        return [{"mp": one} for one in (self.mate, self.peer, self.diag)]

    def copy(self, src, dst, spot, target, arrival=None):
        arrival = spot if arrival is None else arrival
        return remote(src, dst, self.send.at[spot], self.recv.at[arrival], {"mp": target})

    def exchange(self, gath, part, tick=lambda weight: None, fills=(), late=False):
        core, mate, other = self.core, self.mate, 1 - self.core

        def same(rows, spot, target):
            return self.copy(gath.at[rows], gath.at[rows], spot, target)

        def relayed(which):
            rows = half_rows(core, self.far + which)
            same(rows, 1 + which, self.peer).wait_recv()
            one = same(rows, 3 + which, mate)
            one.start()
            sent.append(one)

        sent = [same(image_rows(self.me), 0, mate)]
        sent[0].start()
        across = [
            same(half_rows(core, self.near + which), 1 + which, self.peer) for which in (0, 1)
        ]
        pl.when(core == 0)(across[0].start)
        same(image_rows(mate), 0, mate).wait_recv()
        pl.when(core == 1)(across[0].start)
        across[1].start()
        sent += across
        tick(2)
        self.acc[...] = part(self.me)
        tick(0.4)
        relayed(0)
        near = self.copy(self.near_sums.at[0], self.near_sums.at[1], 5, mate)

        def near_part():
            self.near_sums[0] = part(mate).astype(LOW)
            near.start()
            sent.append(near)
            tick(0.4)

        if not late:
            near_part()
        for which in (0, 1):
            image = self.far + which
            same(half_rows(other, image), 3 + which, mate).wait_recv()
            tick(1.5)
            self.far_acc[...] = part(image)
            self.mixed_sums[2 * which] = self.far_acc[half_rows(other)].astype(LOW)
            mixed = self.copy(
                self.mixed_sums.at[2 * which], self.mixed_sums.at[2 * which + 1], 6 + which, mate
            )
            mixed.start()
            if which == 0:
                relayed(1)
            tick(0.4)
            mixed.wait_recv()
            self.out_sums[which] = (
                self.far_acc[half_rows(core)] + self.mixed_sums[2 * which + 1].astype(FULL)
            ).astype(LOW)
            out = self.copy(
                self.out_sums.at[which], self.far_sums.at[half_rows(core)], 8 + which, image, 8 + core
            )
            out.start()
            sent += [mixed, out]
            tick(1.3)
        if late:
            near_part()
        for fill in fills:
            fill()
            tick(0.6)
        near.wait_recv()
        self.acc[...] += self.near_sums[1].astype(FULL)
        for half in (0, 1):
            self.copy(
                self.out_sums.at[0], self.far_sums.at[half_rows(half)], 8, self.peer, 8 + half
            ).wait_recv()
        for one in sent:
            one.wait_send()
        return self.acc[...] + self.far_sums[...].astype(FULL)


def group_scratch(width):
    return [
        pltpu.VMEM((ROWS, width), FULL),
        pltpu.VMEM((ROWS, width), FULL),
        pltpu.VMEM((2, ROWS, width), LOW),
        pltpu.VMEM((4, HALF, width), LOW),
        pltpu.VMEM((ROWS, width), LOW),
        pltpu.VMEM((2, HALF, width), LOW),
        pltpu.SemaphoreType.DMA((COPIES,)),
        pltpu.SemaphoreType.DMA((COPIES,)),
    ]


class Swap:
    def __init__(self, count, scratch):
        self.count = count
        self.src, self.dst, self.flat, self.send, self.recv = scratch
        self.me = lax.axis_index("dp")
        self.each = self.flat.shape[0] // count
        self.whole = self.each % 16 == 0

    def others(self):
        return [{"dp": lax.rem(self.me + shift, self.count)} for shift in range(1, self.count)]

    def spot(self, ref, index):
        if self.whole:
            return ref.at[pl.ds(pl.multiple_of(index * self.each, 16), self.each)]
        return ref.at[index]

    def copy(self, shift, source, target):
        return remote(
            self.spot(self.src, target), self.spot(self.dst, source),
            self.send.at[shift], self.recv.at[shift], {"dp": target},
        )

    def start(self, values):
        if self.whole:
            self.src[...] = values
        else:
            for index in range(self.count):
                self.src[index] = values[index * self.each : (index + 1) * self.each].astype(FULL)
        order = sorted(range(1, self.count), key=lambda shift: -min(shift, self.count - shift))
        for shift in order:
            self.copy(shift, self.me, lax.rem(self.me + shift, self.count)).start()
        if self.whole:
            rows = pl.ds(pl.multiple_of(self.me * self.each, 16), self.each)
            self.dst[rows] = self.src[rows]
        else:
            self.dst[self.me] = self.src[self.me]

    def arrive(self):
        for shift in range(1, self.count):
            source = lax.rem(self.me + self.count - shift, self.count)
            self.copy(shift, source, source).wait_recv()
        if self.whole:
            return self.dst[...].astype(FULL)
        for index in range(self.count):
            self.flat[index * self.each : (index + 1) * self.each] = self.dst[index]
        return self.flat[...]

    def finish(self):
        for shift in range(1, self.count):
            self.copy(shift, self.me, lax.rem(self.me + shift, self.count)).wait_send()


def swap_scratch(rows, width, count):
    each = rows // count
    block = (rows, width) if each % 16 == 0 else (count, each, width)
    kind = LOW if each % 16 == 0 else FULL
    return [
        pltpu.VMEM(block, kind),
        pltpu.VMEM(block, kind),
        pltpu.VMEM((rows, width), FULL),
        pltpu.SemaphoreType.DMA((count,)),
        pltpu.SemaphoreType.DMA((count,)),
    ]


def placed(slot_ref):
    length = slot_ref.shape[1]
    slots = lax.broadcasted_iota(jnp.int32, (length, length), 0)
    return jnp.where(slots == slot_ref[...], 1.0, 0.0).astype(LOW)


def as_row(ref):
    return ref[...].reshape(1, ref.shape[0])


def pad_into(ref, src):
    ref[...] = jnp.zeros(ref.shape, ref.dtype)
    ref[0 : src.shape[0]] = src[...]


def weight_loads(loads, depth, wqkv, wout, refs):
    wqkv_any, wout_any = refs
    heads = wout_any.shape[1]
    made = [loads.start(wout_any.at[depth], wout.at[pl.ds(0, heads)])]
    for kind in range(3):
        made.append(loads.start(wqkv_any.at[depth, kind], wqkv.at[pl.ds(kind * LANES, heads)]))
    return made


def clear_spare(wqkv, wout, heads):
    width = wout.shape[1]
    wout[heads:LANES] = jnp.zeros((LANES - heads, width), LOW)
    for kind in range(3):
        wqkv[kind * LANES + heads : (kind + 1) * LANES] = jnp.zeros((LANES - heads, width), LOW)


def forward_kernel(
    caption_counts, region_counts,
    features, boxes_ref, w_box_ref, gain_ref, enc_ref, cap_ref, slot_ref,
    b_qv, b_up, row_biases, norm_gains,
    feat_any, wqkv_any, wout_any, wup_any, wdown_any,
    x_out, pre_out, u_out, v_out, ga_out, qkv_out, p_out, ctx_out, hid_out, act_out, slope_out,
    w_feat, wqkv, wout, wup, wdown, biases, boxes, w_box, key_rows,
    ga, qkv, weights, ctx, hid, act, slope, u_buf, v_buf, x_buf, load_sem, save_sem, *scratch, count
):
    group = Group(scratch[:8])
    swap = Swap(count, scratch[8:])
    me = group.me
    heads = wout_any.shape[1]
    loads, saves = Loads(load_sem), Loads(save_sem)
    feat_load = loads.start(feat_any, w_feat)
    for depth in range(LAYERS):
        clear_spare(wqkv.at[depth], wout.at[depth], heads)
    attend_loads, feed_loads = [], []
    for depth in range(LAYERS):
        attend_loads.append(
            weight_loads(loads, depth, wqkv.at[depth], wout.at[depth], (wqkv_any, wout_any))
        )
        feed_loads.append(
            [
                loads.start(wup_any.at[depth], wup.at[depth]),
                loads.start(wdown_any.at[depth], wdown.at[depth]),
            ]
        )
    greet(group.others() + swap.others())

    pad_into(boxes, boxes_ref)
    pad_into(w_box, w_box_ref)
    feat_load.wait()
    pre = dot_nn(features[...], w_feat[...])
    pre += lax.dot_general(
        boxes[...], w_box[...], (((0,), (0,)), ((), ())),
        precision=lax.Precision.HIGHEST, preferred_element_type=FULL,
    )
    pre += enc_ref[0:1]
    hat, _ = normed_rows(pre)
    swap.start((hat * as_row(gain_ref) + enc_ref[1:2]).astype(LOW))
    pre_out[...] = pre
    x_buf[0:CAP] = cap_ref[...].astype(FULL)
    place = placed(slot_ref)
    biases[...] = jnp.zeros(biases.shape, FULL)
    for depth in range(LAYERS):
        biases[depth, 0:1, 0:heads] = b_qv[depth, 0:1]
        biases[depth, 0:1, 2 * LANES : 2 * LANES + heads] = b_qv[depth, 1:2]
    spots = lax.broadcasted_iota(jnp.int32, (8, SEQ), 1)
    for image in range(GROUP):
        seen = jnp.where(
            spots < CAP, spots - caption_counts[image], spots - CAP - region_counts[image]
        )
        key_rows[image] = jnp.where(seen < 0, 0.0, -1e30)
    masks = head_masks()
    x_buf[CAP:] = dot_nn(place, swap.arrive().astype(LOW))

    for depth in range(LAYERS):

        def attend(image):
            rows = image_rows(image)
            low = (dot_nt(ga[depth, rows], wqkv[depth]) + biases[depth, 0:1]).astype(LOW)
            qkv[depth, rows] = low
            queries, keys_low, values_low = (
                low[:, :LANES], low[:, LANES : 2 * LANES], low[:, 2 * LANES :],
            )
            total = jnp.zeros((ROWS, LANES), FULL)
            for head in range(3):
                scores = dot_nt(queries * masks[head], keys_low) * HD ** (-0.5)
                scores += key_rows[image, 0:1]
                raised = jnp.exp(scores - jnp.max(scores, axis=-1, keepdims=True))
                prob = (raised / jnp.sum(raised, axis=-1, keepdims=True)).astype(LOW)
                weights[depth, image, head] = prob
                total += dot_nn(prob, values_low * masks[head])
            low_ctx = total.astype(LOW)
            ctx[depth, rows] = low_ctx
            return dot_nn(low_ctx, wout[depth])

        def feed(image):
            rows = image_rows(image)
            pre = dot_nn(hid[depth, rows], wup[depth]) + b_up[depth : depth + 1]
            half = 0.5 * (1.0 + lax.erf(pre * 2.0 ** (-0.5)))
            low = (pre * half).astype(LOW)
            act[depth, rows] = low
            slope[depth, rows] = (
                half + pre * jnp.exp(-0.5 * pre * pre) * 0.3989422804014327
            ).astype(LOW)
            return dot_nn(low, wdown[depth])

        states = x_buf[...]
        ga[depth, image_rows(me)] = states.astype(LOW)
        for one in attend_loads[depth]:
            one.wait()
        total = group.exchange(ga.at[depth], attend)
        for src, dst in ((ga, ga_out), (qkv, qkv_out), (weights, p_out), (ctx, ctx_out)):
            saves.start(src.at[depth], dst.at[depth])
        pre_attn = x_buf[...] + total + row_biases[depth, 0:1]
        hat, _ = normed_rows(pre_attn)
        normed = hat * norm_gains[depth, 0:1] + row_biases[depth, 1:2]
        hid[depth, image_rows(me)] = normed.astype(LOW)
        u_buf[depth] = pre_attn
        saves.start(u_buf.at[depth], u_out.at[depth])
        x_buf[...] = normed
        for one in feed_loads[depth]:
            one.wait()
        total = group.exchange(hid.at[depth], feed, late=True)
        for src, dst in ((hid, hid_out), (act, act_out), (slope, slope_out)):
            saves.start(src.at[depth], dst.at[depth])
        pre_ffn = x_buf[...] + total + row_biases[depth, 2:3]
        v_buf[depth] = pre_ffn
        saves.start(v_buf.at[depth], v_out.at[depth])
        hat, _ = normed_rows(pre_ffn)
        x_buf[...] = hat * norm_gains[depth, 1:2] + row_biases[depth, 3:4]

    x_out[...] = x_buf[...]
    swap.finish()
    for depth in range(LAYERS):
        for place, (src, dst) in enumerate(
            (
                (ga, ga_out), (qkv, qkv_out), (weights, p_out), (ctx, ctx_out), (u_buf, u_out),
                (hid, hid_out), (act, act_out), (slope, slope_out), (v_buf, v_out),
            )
        ):
            pltpu.make_async_copy(
                src.at[depth], dst.at[depth], save_sem.at[9 * depth + place]
            ).wait()


def forward(
    count, caption_counts, region_counts, features, boxes, w_box, gain, enc, captions, slots,
    b_qv, b_up, row_biases, norm_gains, w_feat, wqkv, wout, wup, wdown,
):
    width = captions.shape[1]
    hidden = wup.shape[2]
    rows = features.shape[0]
    group = GROUP * ROWS
    saved = [
        ((LAYERS, group, width), LOW),
        ((LAYERS, group, 3 * LANES), LOW),
        ((LAYERS, GROUP, 3, ROWS, ROWS), LOW),
        ((LAYERS, group, LANES), LOW),
        ((LAYERS, group, width), LOW),
        ((LAYERS, group, hidden), LOW),
        ((LAYERS, group, hidden), LOW),
    ]
    kept = ((LAYERS, ROWS, width), FULL)
    shapes = [((ROWS, width), FULL), ((rows, width), FULL), kept, kept] + saved
    vmem = pl.BlockSpec(memory_space=pltpu.VMEM)
    smem = pl.BlockSpec(memory_space=pltpu.SMEM)
    loose = pl.BlockSpec(memory_space=pl.ANY)
    return pl.pallas_call(
        functools.partial(forward_kernel, count=count),
        out_shape=[jax.ShapeDtypeStruct(*one) for one in shapes],
        in_specs=[smem] * 2 + [vmem] * 11 + [loose] * 5,
        out_specs=[vmem] * 2 + [loose] * 9,
        scratch_shapes=[
            pltpu.VMEM(w_feat.shape, LOW),
            pltpu.VMEM((LAYERS, 3 * LANES, width), LOW),
            pltpu.VMEM((LAYERS, LANES, width), LOW),
            pltpu.VMEM(wup.shape, LOW),
            pltpu.VMEM(wdown.shape, LOW),
            pltpu.VMEM((LAYERS, 8, 3 * LANES), FULL),
            pltpu.VMEM((8, rows), FULL),
            pltpu.VMEM((8, width), FULL),
            pltpu.VMEM((GROUP, 8, SEQ), FULL),
        ]
        + [pltpu.VMEM(*one) for one in saved]
        + [pltpu.VMEM(*kept), pltpu.VMEM(*kept), pltpu.VMEM((ROWS, width), FULL)]
        + [pltpu.SemaphoreType.DMA((1 + 6 * LAYERS,)), pltpu.SemaphoreType.DMA((9 * LAYERS,))]
        + group_scratch(width)
        + swap_scratch(rows, width, count),
        compiler_params=pltpu.CompilerParams(
            collective_id=0, has_side_effects=True, vmem_limit_bytes=60 * 2**20
        ),
    )(
        caption_counts, region_counts, features, boxes, w_box, gain, enc, captions, slots,
        b_qv, b_up, row_biases, norm_gains, w_feat, wqkv, wout, wup, wdown,
    )


def ring_places(count):
    me = lax.axis_index("dp")
    half = count // 2

    def device(place):
        side = place // half
        depth = place + side * (count - 1 - 2 * place)
        return 2 * depth + side

    side = lax.rem(me, 2)
    depth = me // 2
    place = depth + side * (count - 1 - 2 * depth)
    return place, device(lax.rem(place + 1, count)), device(lax.rem(place + count - 1, count))


def ring_rows(length, count):
    each = -(-length // (16 * count))
    first = 16 * (each // 2)
    sizes = (first, 16 * each - first) if first else (16 * each,)
    return count * each * 16, sizes


class Ring:
    def __init__(self, count, places, pack, lands, sems, passed=None, flush=None):
        self.count, self.last = count, count - 1
        self.place, self.after, self.before = places
        self.pack, self.lands, self.sems = pack, lands, sems
        self.sizes = [land.shape[1] for land in lands]
        self.ways = range(len(self.sizes))
        self.taken, self.due = 0, 0
        self.passed, self.flush = passed, flush

    def chunk(self, way, offset):
        spot = lax.rem(self.place + (offset if way else -offset) + 2 * self.count, self.count)
        start = spot * sum(self.sizes) + way * self.sizes[0]
        return pl.ds(pl.multiple_of(start, 16), self.sizes[way])

    def copy(self, phase, way, step, rows=None):
        if phase == 0:
            src = self.pack.at[self.chunk(way, 0)] if step == 0 else self.lands[way].at[step - 1]
            dst = self.lands[way].at[step]
        else:
            if rows is None:
                rows = self.chunk(way, step - 1)
            src = self.pack.at[rows]
            dst = self.pack.at[rows]
        return remote(
            src, dst, self.sems.at[2 * phase, way, step], self.sems.at[2 * phase + 1, way, step],
            {"dp": self.before if way else self.after},
        )

    def running(self):
        return self.taken <= 2 * self.last

    def step(self):
        index, last = self.taken, self.last
        for way in self.ways:
            if index == 0:
                self.copy(0, way, 0).start()
            elif index <= last:
                done = index - 1
                self.copy(0, way, done).wait_recv()
                if done == 0:
                    self.copy(0, way, 0).wait_send()
                rows = self.chunk(way, done + 1)
                added = (self.lands[way][done].astype(FULL) + self.pack[rows].astype(FULL)).astype(LOW)
                if index < last:
                    self.lands[way][done] = added
                    self.copy(0, way, index).start()
                else:
                    self.pack[rows] = added
                    self.copy(1, way, 0).start()
                    self.pass_on(rows)
            else:
                done = index - last - 1
                rows = self.chunk(way, done)
                self.copy(1, way, done, rows).wait_recv()
                if done + 1 < last:
                    self.copy(1, way, done + 1).start()
                self.pass_on(rows)
        self.taken += 1
        if not self.running() and self.flush is not None:
            self.flush()

    def pass_on(self, rows):
        if self.passed is not None:
            self.passed(rows)

    def finish(self):
        for phase in range(2):
            for way in self.ways:
                for step in range(1 - phase, self.last):
                    self.copy(phase, way, step).wait_send()


class Clock:
    def __init__(self):
        self.now, self.link, self.rings = 0, 0, []

    def add(self, ring):
        ring.due = self.now
        self.rings.append(ring)

    def running(self):
        return [ring for ring in self.rings if ring.running()]

    def visit(self, ring):
        self.now = max(self.now, ring.due)
        ring.step()
        self.link = max(self.link, self.now) + max(ring.sizes) * 0.036
        ring.due = self.link + 2

    def tick(self, weight):
        self.now += weight
        for ring in sorted(self.running(), key=lambda one: one.due):
            if ring.due <= self.now:
                self.visit(ring)

    def drain(self, first):
        while self.running():
            others = [ring for ring in self.running() if ring is not first]
            later = min(others, key=lambda one: one.due + 0.5 * one.taken, default=None)
            if first.running() and (later is None or later.due > first.due or self.link > first.due - 1):
                self.visit(first)
            else:
                self.visit(later)


def backward_kernel(
    cot_ref, slot_ref, boxes_ref, gain_ref, pre_ref, norm_gains,
    wqkv_any, wout_any, wup_any, wdown_any, u_any, v_any,
    ga_any, qkv_any, p_any, ctx_any, hid_any, act_any, slope_any, feat_any, w_feat_any,
    cap_out, back_out, box_out, gain_out, enc_out, qv_out, up_sum_out, norms_out, rows_out,
    down_out, up_out, out_out, mixed_out, feat_out,
    wqkv, wout, wup, wdown, u_buf, v_buf,
    ga, qkv, weights, ctx, hid, act, slope, low_e, d_up, low_f, d_mixed,
    keep, small, small_in, extra_sum, extra_in, down_pack, up_pack, thin_pack, ring_sems,
    features, boxes, feat_in, feat_send, feat_pack, feat_sems,
    send, recv, small_send, small_recv, load_sem, local_sem, *scratch, count, ways
):
    group = Group(scratch[:8])
    swap = Swap(count, scratch[8:13])
    lands = list(scratch[13:])
    down_lands, up_lands, thin_lands, feat_lands = (
        [lands.pop(0) for _ in range(number)] for number in ways
    )
    me, mate, peer, diag = group.me, group.mate, group.peer, group.diag
    width = keep.shape[1]
    heads = wout_any.shape[1]
    hidden = act.shape[1]
    loads, local = Loads(load_sem), Loads(local_sem)

    def feed_load(depth):
        return [
            loads.start(src.at[depth], dst)
            for src, dst in (
                (v_any, v_buf), (wdown_any, wdown), (slope_any, slope), (wup_any, wup),
                (act_any, act), (hid_any, hid),
            )
        ]

    def attend_load(depth):
        return [
            loads.start(src.at[depth], dst)
            for src, dst in (
                (u_any, u_buf), (p_any, weights), (qkv_any, qkv), (ctx_any, ctx), (ga_any, ga),
            )
        ] + weight_loads(loads, depth, wqkv, wout, (wqkv_any, wout_any))

    feed_waits = feed_load(LAYERS - 1)
    clear_spare(wqkv, wout, heads)
    attend_waits = attend_load(LAYERS - 1)
    greet(group.others() + swap.others())
    places = ring_places(count)

    def down_flush(depth):
        local.start(down_pack.at[depth, pl.ds(0, hidden)], down_out.at[depth])

    def up_flush(depth):
        local.start(up_pack.at[depth, pl.ds(0, width)], up_out.at[depth])

    def thin_flush(depth):
        local.start(thin_pack.at[depth, pl.ds(0, heads)], out_out.at[depth])
        for kind in range(3):
            rows = pl.ds(heads * (kind + 1), heads)
            local.start(thin_pack.at[depth, rows], mixed_out.at[depth, kind])

    def rings(spot, pack, own_lands, flush):
        return [
            Ring(
                count, places, pack.at[depth], [one.at[depth] for one in own_lands],
                ring_sems.at[spot, depth], flush=functools.partial(flush, depth),
            )
            for depth in range(LAYERS)
        ]

    downs = rings(0, down_pack, down_lands, down_flush)
    ups = rings(1, up_pack, up_lands, up_flush)
    thins = rings(2, thin_pack, thin_lands, thin_flush)
    clock = Clock()
    tick = clock.tick
    masks = head_masks()

    for depth in reversed(range(LAYERS)):

        def feed_back(image):
            rows = image_rows(image)
            low = (dot_nt(low_e[rows], wdown[...]) * slope[rows].astype(FULL)).astype(LOW)
            d_up[rows] = low
            tick(0.8)
            return dot_nt(low, wup[...])

        def attend_back(image):
            rows = image_rows(image)
            d_ctx = dot_nt(low_f[rows], wout[...]).astype(LOW)
            low = qkv[rows]
            queries, keys_low, values_low = (
                low[:, :LANES], low[:, LANES : 2 * LANES], low[:, 2 * LANES :],
            )
            d_q = jnp.zeros((ROWS, LANES), FULL)
            d_k = jnp.zeros((ROWS, LANES), FULL)
            d_v = jnp.zeros((ROWS, LANES), FULL)
            for head in range(3):
                own = d_ctx * masks[head]
                prob_low = weights[image, head]
                d_v += dot_tn(prob_low, own)
                d_prob = dot_nt(own, values_low)
                prob = prob_low.astype(FULL)
                meant = jnp.sum(prob * d_prob, axis=-1, keepdims=True)
                d_score = (prob * (d_prob - meant)).astype(LOW)
                d_q += dot_nn(d_score, keys_low * masks[head])
                d_k += dot_tn(d_score, queries * masks[head])
                tick(1.2)
            scaling = HD ** (-0.5)
            d_mixed[rows, 0:LANES] = (d_q * scaling).astype(LOW)
            d_mixed[rows, LANES : 2 * LANES] = (d_k * scaling).astype(LOW)
            d_mixed[rows, 2 * LANES : 3 * LANES] = d_v.astype(LOW)
            return dot_nn(d_mixed[rows], wqkv[...])

        def down_fill(start):
            def fill():
                down_pack[depth, start : start + LANES] = dot_tn(
                    act[:, start : start + LANES], low_e[...]
                ).astype(LOW)

            return fill

        def up_fill(start):
            def fill():
                up_pack[depth, start : start + LANES] = dot_tn(
                    hid[:, start : start + LANES], d_up[...]
                ).astype(LOW)

            return fill

        def out_fill():
            thin_pack[depth, 0:heads] = dot_tn(ctx[...], low_f[...])[:heads].astype(LOW)

        def mixed_fill(kind):
            def fill():
                base = heads * (kind + 1)
                made = dot_tn(d_mixed[:, kind * LANES : (kind + 1) * LANES], ga[...])
                thin_pack[depth, base : base + heads] = made[:heads].astype(LOW)

            return fill

        def small_copy(spot, target):
            return remote(
                small.at[depth], small_in.at[depth, spot],
                small_send.at[depth, spot], small_recv.at[depth, spot], {"mp": target},
            )

        first, second = small_copy(0, mate), small_copy(1, peer)

        def small_fill():
            first.wait_recv()
            first.wait_send()
            small[depth] += small_in[depth, 0]
            second.start()

        gradient = cot_ref[...].astype(FULL) if depth == LAYERS - 1 else keep[...]
        feed_waits[0].wait()
        d_pre, hat = normed_back(gradient, v_buf[...], norm_gains[depth, 1:2])
        low_e[image_rows(me)] = d_pre.astype(LOW)
        keep[...] = d_pre
        small[depth] = jnp.zeros((8, width), FULL)
        small[depth, 1:2] = row_sum(gradient * hat)
        small[depth, 4:5] = row_sum(d_pre)
        small[depth, 5:6] = row_sum(gradient)
        for one in feed_waits[1:]:
            one.wait()
        total = group.exchange(
            low_e, feed_back, tick,
            [down_fill(start) for start in range(0, hidden, LANES)]
            + [functools.partial(clock.add, downs[depth])]
            + [up_fill(start) for start in range(0, width, LANES)]
            + [functools.partial(clock.add, ups[depth])],
        )
        tick(2)
        b_up_sum = row_sum(d_up[...].astype(FULL))
        if depth:
            feed_waits = feed_load(depth - 1)
        gradient = keep[...] + total
        if depth < LAYERS - 1:
            pass
        attend_waits[0].wait()
        d_pre, hat = normed_back(gradient, u_buf[...], norm_gains[depth, 0:1])
        low_f[image_rows(me)] = d_pre.astype(LOW)
        keep[...] = d_pre
        small[depth, 0:1] = row_sum(gradient * hat)
        small[depth, 2:3] = row_sum(d_pre)
        small[depth, 3:4] = row_sum(gradient)
        first.start()
        for one in attend_waits[1:]:
            one.wait()
        total = group.exchange(
            low_f, attend_back, tick,
            [small_fill, out_fill]
            + [mixed_fill(kind) for kind in range(3)]
            + [functools.partial(clock.add, thins[depth])],
            late=True,
        )
        tick(2)
        second.wait_recv()
        second.wait_send()
        small[depth] += small_in[depth, 1]
        small[depth, 6:7] = b_up_sum
        small[depth, 7:8] = row_sum(d_mixed[...].astype(FULL))
        if depth:
            attend_waits = attend_load(depth - 1)
        keep[...] += total

    cap_out[...] = keep[0:CAP]
    place = placed(slot_ref)
    swap.start(dot_tn(place, keep[CAP:].astype(LOW)).astype(LOW))
    span = act.shape[0]
    feat_loads = [
        loads.start(feat_any, features),
        loads.start(w_feat_any.at[pl.ds(0, span)], act),
        loads.start(w_feat_any.at[pl.ds(span, span)], slope),
    ]
    pad_into(boxes, boxes_ref)
    each = feat_send.shape[0]
    gradient = swap.arrive()
    tick(6)
    d_pre, hat = normed_back(gradient, pre_ref[...], as_row(gain_ref))
    low = d_pre.astype(LOW)
    feat_loads[0].wait()

    def product(ref, spot):
        columns = pl.ds(pl.multiple_of(spot * each, 128), each)
        ref[0:each] = dot_tn(features[:, columns], low).astype(LOW)

    def copy(src, dst, spot, target):
        return remote(src, dst, send.at[spot], recv.at[spot], {"mp": target})

    span_rows = pl.ds(0, each)
    to_mate = [
        copy(low_e.at[span_rows], feat_in.at[0], 0, mate),
        copy(d_up.at[span_rows], feat_in.at[1], 1, mate),
    ]
    product(low_e, diag)
    to_mate[0].start()
    product(low_f, peer)
    tick(1.5)
    to_mate[0].wait_recv()
    feat_send[...] = (low_f[0:each].astype(FULL) + feat_in[0].astype(FULL)).astype(LOW)
    to_peer = copy(feat_send, feat_in.at[2], 2, peer)
    to_peer.start()
    tick(2)
    rounded = low.astype(FULL)
    extra_sum[...] = jnp.concatenate(
        [
            lax.dot_general(
                boxes[...], rounded, (((1,), (0,)), ((), ())),
                precision=lax.Precision.HIGHEST, preferred_element_type=FULL,
            ),
            row_sum(gradient * hat),
            row_sum(rounded),
            row_sum(gradient),
            jnp.zeros((5, width), FULL),
        ],
        axis=0,
    )
    extras = [copy(extra_sum, extra_in.at[spot], 6 + spot, target) for spot, target in ((0, mate), (1, peer))]
    extras[0].start()
    product(d_up, mate)
    to_mate[1].start()
    tick(1)
    product(hid, me)
    tick(1)
    extras[0].wait_recv()
    extras[0].wait_send()
    extra_sum[...] += extra_in[0]
    extras[1].start()
    feat_loads[1].wait()
    back_out[:, 0:span] = dot_nt(low, act[...])
    tick(1)
    feat_loads[2].wait()
    back_out[:, span:] = dot_nt(low, slope[...])
    to_mate[1].wait_recv()
    own = hid[0:each].astype(FULL) + feat_in[1].astype(FULL)
    hid[0:each] = own.astype(LOW)
    tick(1.5)
    extras[1].wait_recv()
    extras[1].wait_send()
    base = each + 16
    feat_pack[each:base] = (extra_sum[...] + extra_in[1]).astype(LOW)
    for depth in range(LAYERS):
        feat_pack[base : base + 16] = jnp.concatenate(
            [small[depth], jnp.zeros((8, width), FULL)], axis=0
        ).astype(LOW)
        base += 16
    feat_rows = feat_pack.shape[0]
    if feat_rows > base:
        feat_pack[base:] = jnp.zeros((feat_rows - base, width), LOW)
    for _ in range(6):
        tick(2)
    to_peer.wait_recv()
    feat_pack[0:each] = (hid[0:each].astype(FULL) + feat_in[2].astype(FULL)).astype(LOW)

    def ours(spot, start, size):
        return feat_out.at[pl.ds(pl.multiple_of(spot * each + start, 16), size)]

    def spread(rows):
        @pl.when(rows.start < each)
        def _():
            for spot, target in ((3, peer), (4, mate)):
                copy(feat_pack.at[rows], ours(me, rows.start, rows.size), spot, target).start()

    feat = Ring(count, places, feat_pack, feat_lands, feat_sems, spread)
    clock.add(feat)
    clock.drain(feat)
    local.start(feat_pack.at[span_rows], ours(me, 0, each))
    base = each
    box_out[...] = feat_pack[base : base + 16].astype(FULL)[0:4]
    gain_out[...] = feat_pack[base : base + 16].astype(FULL)[8:9].reshape(width)
    enc_out[...] = feat_pack[base : base + 16].astype(FULL)[9:11]
    for depth in range(LAYERS):
        base += 16
        sums = feat_pack[base : base + 16].astype(FULL)
        norms_out[depth] = sums[0:2]
        rows_out[depth] = sums[2:6]
        up_sum_out[depth : depth + 1] = sums[6:7]
        qv_out[depth, 0:1] = sums[7:8, 0:heads]
        qv_out[depth, 1:2] = sums[7:8, 2 * LANES : 2 * LANES + heads]
    copy(feat_send, ours(peer, 0, each), 3, peer).wait_recv()
    relay = copy(ours(peer, 0, each), ours(peer, 0, each), 5, mate)
    relay.start()
    copy(feat_send, ours(mate, 0, each), 4, mate).wait_recv()
    copy(feat_send, ours(diag, 0, each), 5, mate).wait_recv()
    for spot in (3, 4):
        copy(feat_send, ours(me, 0, each), spot, mate).wait_send()
    for one in to_mate + [to_peer, relay]:
        one.wait_send()
    for ring in downs + ups + thins + [feat]:
        ring.finish()
    swap.finish()
    for one in local.made:
        one.wait()


def backward(
    count, cotangent, slots, boxes, gain, pre, norm_gains, wqkv, wout, wup, wdown, kept,
    features, w_feat,
):
    width = cotangent.shape[1]
    rows, columns = features.shape
    hidden = wup.shape[2]
    heads = wout.shape[1]
    group = GROUP * ROWS
    each = columns // GROUP
    down_rows, down_sizes = ring_rows(hidden, count)
    up_rows, up_sizes = ring_rows(width, count)
    thin_rows, thin_sizes = ring_rows(GROUP * heads, count)
    feat_rows, feat_sizes = ring_rows(each + 16 + 16 * LAYERS, count)

    def ring_sems(*lead):
        return pltpu.SemaphoreType.DMA(lead + (4, 2, count - 1))

    vmem = pl.BlockSpec(memory_space=pltpu.VMEM)
    loose = pl.BlockSpec(memory_space=pl.ANY)
    packs = [((LAYERS, size, width), LOW) for size in (down_rows, up_rows, thin_rows)]
    shapes = [
        ((CAP, width), FULL),
        ((rows, columns), FULL),
        ((4, width), FULL),
        ((width,), FULL),
        ((2, width), FULL),
        ((LAYERS, 2, heads), FULL),
        ((LAYERS, hidden), FULL),
        ((LAYERS, 2, width), FULL),
        ((LAYERS, 4, width), FULL),
        ((LAYERS, hidden, width), LOW),
        ((LAYERS, width, hidden), LOW),
        ((LAYERS, heads, width), LOW),
        ((LAYERS, 3, heads, width), LOW),
        ((columns, width), LOW),
    ]
    return pl.pallas_call(
        functools.partial(
            backward_kernel,
            count=count,
            ways=[len(one) for one in (down_sizes, up_sizes, thin_sizes, feat_sizes)],
        ),
        out_shape=[jax.ShapeDtypeStruct(*one) for one in shapes],
        in_specs=[vmem] * 6 + [loose] * 15,
        out_specs=[vmem] * 9 + [loose] * 5,
        scratch_shapes=[
            pltpu.VMEM((3 * LANES, width), LOW),
            pltpu.VMEM((LANES, width), LOW),
            pltpu.VMEM(wup.shape[1:], LOW),
            pltpu.VMEM(wdown.shape[1:], LOW),
            pltpu.VMEM((ROWS, width), FULL),
            pltpu.VMEM((ROWS, width), FULL),
        ]
        + [pltpu.VMEM(one.shape[1:], one.dtype) for one in kept[2:]]
        + [
            pltpu.VMEM((group, width), LOW),
            pltpu.VMEM((group, hidden), LOW),
            pltpu.VMEM((group, width), LOW),
            pltpu.VMEM((group, 3 * LANES), LOW),
            pltpu.VMEM((ROWS, width), FULL),
            pltpu.VMEM((LAYERS, 8, width), FULL),
            pltpu.VMEM((LAYERS, 2, 8, width), FULL),
            pltpu.VMEM((16, width), FULL),
            pltpu.VMEM((2, 16, width), FULL),
        ]
        + [pltpu.VMEM(*one) for one in packs]
        + [ring_sems(3, LAYERS)]
        + [
            pltpu.VMEM(features.shape, LOW),
            pltpu.VMEM((8, rows), FULL),
            pltpu.VMEM((3, each, width), LOW),
            pltpu.VMEM((each, width), LOW),
            pltpu.VMEM((feat_rows, width), LOW),
            ring_sems(),
            pltpu.SemaphoreType.DMA((8,)),
            pltpu.SemaphoreType.DMA((8,)),
            pltpu.SemaphoreType.DMA((LAYERS, 2)),
            pltpu.SemaphoreType.DMA((LAYERS, 2)),
            pltpu.SemaphoreType.DMA((15 * LAYERS + 3,)),
            pltpu.SemaphoreType.DMA((1 + 6 * LAYERS,)),
        ]
        + group_scratch(width)
        + swap_scratch(rows, width, count)
        + [
            pltpu.VMEM((LAYERS, count - 1, size, width), LOW) for size in down_sizes + up_sizes + thin_sizes
        ]
        + [pltpu.VMEM((count - 1, size, width), LOW) for size in feat_sizes],
        compiler_params=pltpu.CompilerParams(
            collective_id=1, has_side_effects=True, vmem_limit_bytes=62 * 2**20
        ),
    )(
        cotangent, slots, boxes, gain, pre, norm_gains, wqkv, wout, wup, wdown, *kept,
        features, w_feat,
    )


def on_device(
    captions,
    features,
    region_boxes,
    caption_counts,
    region_counts,
    slot_map,
    w_feat,
    w_box,
    enc_gain,
    enc_vectors,
    w_qkv,
    b_qv,
    w_out,
    w_up,
    b_up,
    w_down,
    norm_gains,
    row_biases,
    cotangent,
):
    count = lax.axis_size("dp")
    wqkv = w_qkv.transpose(0, 2, 3, 1)
    layer_output, enc_pre, *kept = forward(
        count, caption_counts, region_counts, features, region_boxes, w_box, enc_gain, enc_vectors,
        captions, slot_map, b_qv, b_up, row_biases, norm_gains, w_feat, wqkv, w_out, w_up, w_down,
    )
    (
        caption_grad, feature_grad, box_sum, gain_sum, enc_sum, qv_sum, up_sum, norm_sum, row_sums,
        down, up, out, mixed, feat,
    ) = backward(
        count, cotangent, slot_map, region_boxes, enc_gain, enc_pre, norm_gains, wqkv, w_out, w_up,
        w_down, kept, features, w_feat,
    )
    return (
        layer_output,
        caption_grad,
        feature_grad,
        feat.astype(FULL),
        box_sum,
        gain_sum,
        enc_sum,
        mixed.astype(FULL).transpose(0, 3, 1, 2),
        qv_sum,
        out.astype(FULL),
        up.astype(FULL),
        up_sum,
        down.astype(FULL),
        norm_sum,
        row_sums,
    )


def solution(mesh):
    return jax.shard_map(
        on_device,
        mesh=mesh,
        in_specs=(
            P(("dp", "mp"), None),
            P(("dp", "mp"), None),
            P(None, ("dp", "mp")),
            P("dp"),
            P("dp"),
            P(("dp", "mp"), None),
            P(),
            P(),
            P(),
            P(),
            P(None, None, None, "mp"),
            P(None, None, "mp"),
            P(None, "mp", None),
            P(None, None, "mp"),
            P(None, "mp"),
            P(None, "mp", None),
            P(),
            P(),
            P(("dp", "mp"), None),
        ),
        out_specs=(
            P(("dp", "mp"), None),
            P(("dp", "mp"), None),
            P(("dp", "mp"), None),
            P(),
            P(),
            P(),
            P(),
            P(None, None, None, "mp"),
            P(None, None, "mp"),
            P(None, "mp", None),
            P(None, None, "mp"),
            P(None, "mp"),
            P(None, "mp", None),
            P(),
            P(),
        ),
        check_vma=False,
    )
```

```python
import functools

import jax
import jax.numpy as jnp
from jax import lax
from jax.experimental import pallas as pl
from jax.experimental.pallas import tpu as pltpu
from jax.sharding import PartitionSpec as P

HD = 64
CAP = 128
RPAD = 128
LAYERS = 2
SEQ = 256
ROWS = SEQ
HALF = ROWS // 2
LANES = 256
GROUP = 4
COPIES = 10
LOW, FULL = jnp.bfloat16, jnp.float32
MESH = pl.DeviceIdType.MESH

epsilon = 1e-05


def dot_nn(left, right):
    return jnp.dot(left, right, preferred_element_type=FULL)


def dot_nt(left, right):
    return lax.dot_general(left, right, (((1,), (1,)), ((), ())), preferred_element_type=FULL)


def dot_tn(left, right):
    return lax.dot_general(left, right, (((0,), (0,)), ((), ())), preferred_element_type=FULL)


def row_sum(values):
    return jnp.sum(values, axis=0, keepdims=True)


def normed_rows(values):
    centre = values - jnp.mean(values, axis=-1, keepdims=True)
    spread = jnp.mean(centre * centre, axis=-1, keepdims=True)
    inverse = lax.rsqrt(spread + epsilon)
    return centre * inverse, inverse


def normed_back(gradient, values, gain):
    hat, inverse = normed_rows(values)
    scaled = gradient * gain
    tilt = jnp.mean(scaled * hat, axis=-1, keepdims=True)
    level = jnp.mean(scaled, axis=-1, keepdims=True)
    return inverse * (scaled - level - hat * tilt), hat


def head_masks():
    lane = lax.broadcasted_iota(jnp.int32, (1, LANES), 1)
    return [
        jnp.where((lane >= head * HD) & (lane < head * HD + HD), 1.0, 0.0).astype(LOW)
        for head in range(3)
    ]


def image_rows(image):
    return pl.ds(pl.multiple_of(image * ROWS, ROWS), ROWS)


def half_rows(half, image=0):
    return pl.ds(pl.multiple_of(image * ROWS + half * HALF, HALF), HALF)


def remote(src, dst, send_sem, recv_sem, target):
    return pltpu.make_async_remote_copy(
        src_ref=src,
        dst_ref=dst,
        send_sem=send_sem,
        recv_sem=recv_sem,
        device_id=target,
        device_id_type=MESH,
    )


def greet(targets):
    barrier = pltpu.get_barrier_semaphore()
    for target in targets:
        pl.semaphore_signal(barrier, inc=1, device_id=target, device_id_type=MESH)
    pl.semaphore_wait(barrier, len(targets))


class Loads:
    def __init__(self, sems):
        self.sems, self.used, self.made = sems, 0, []

    def start(self, src, dst):
        one = pltpu.make_async_copy(src, dst, self.sems.at[self.used])
        self.used += 1
        self.made.append(one)
        one.start()
        return one


class Group:
    def __init__(self, scratch):
        self.me = lax.axis_index("mp")
        self.core = lax.rem(self.me, 2)
        self.mate = self.me + 1 - 2 * self.core
        self.peer = lax.rem(self.me + 2, GROUP)
        self.diag = lax.rem(self.mate + 2, GROUP)
        self.near = self.me - self.core
        self.far = self.peer - self.core
        (
            self.acc, self.far_acc, self.near_sums, self.mixed_sums, self.far_sums, self.out_sums,
            self.send, self.recv,
        ) = scratch

    def others(self):
        return [{"mp": one} for one in (self.mate, self.peer, self.diag)]

    def copy(self, src, dst, spot, target, arrival=None):
        arrival = spot if arrival is None else arrival
        return remote(src, dst, self.send.at[spot], self.recv.at[arrival], {"mp": target})

    def exchange(self, gath, part, tick=lambda weight: None, fills=(), late=False):
        core, mate, other = self.core, self.mate, 1 - self.core

        def same(rows, spot, target):
            return self.copy(gath.at[rows], gath.at[rows], spot, target)

        def relayed(which):
            rows = half_rows(core, self.far + which)
            same(rows, 1 + which, self.peer).wait_recv()
            one = same(rows, 3 + which, mate)
            one.start()
            sent.append(one)

        sent = [same(image_rows(self.me), 0, mate)]
        sent[0].start()
        across = [
            same(half_rows(core, self.near + which), 1 + which, self.peer) for which in (0, 1)
        ]
        pl.when(core == 0)(across[0].start)
        same(image_rows(mate), 0, mate).wait_recv()
        pl.when(core == 1)(across[0].start)
        across[1].start()
        sent += across
        tick(2)
        self.acc[...] = part(self.me)
        tick(0.4)
        relayed(0)
        near = self.copy(self.near_sums.at[0], self.near_sums.at[1], 5, mate)

        def near_part():
            self.near_sums[0] = part(mate).astype(LOW)
            near.start()
            sent.append(near)
            tick(0.4)

        if not late:
            near_part()
        for which in (0, 1):
            image = self.far + which
            same(half_rows(other, image), 3 + which, mate).wait_recv()
            tick(1.5)
            self.far_acc[...] = part(image)
            self.mixed_sums[2 * which] = self.far_acc[half_rows(other)].astype(LOW)
            mixed = self.copy(
                self.mixed_sums.at[2 * which], self.mixed_sums.at[2 * which + 1], 6 + which, mate
            )
            mixed.start()
            if which == 0:
                relayed(1)
            tick(0.4)
            mixed.wait_recv()
            self.out_sums[which] = (
                self.far_acc[half_rows(core)] + self.mixed_sums[2 * which + 1].astype(FULL)
            ).astype(LOW)
            out = self.copy(
                self.out_sums.at[which], self.far_sums.at[half_rows(core)], 8 + which, image, 8 + core
            )
            out.start()
            sent += [mixed, out]
            tick(1.3)
        if late:
            near_part()
        for fill in fills:
            fill()
            tick(0.6)
        near.wait_recv()
        self.acc[...] += self.near_sums[1].astype(FULL)
        for half in (0, 1):
            self.copy(
                self.out_sums.at[0], self.far_sums.at[half_rows(half)], 8, self.peer, 8 + half
            ).wait_recv()
        for one in sent:
            one.wait_send()
        return self.acc[...] + self.far_sums[...].astype(FULL)


def group_scratch(width):
    return [
        pltpu.VMEM((ROWS, width), FULL),
        pltpu.VMEM((ROWS, width), FULL),
        pltpu.VMEM((2, ROWS, width), LOW),
        pltpu.VMEM((4, HALF, width), LOW),
        pltpu.VMEM((ROWS, width), LOW),
        pltpu.VMEM((2, HALF, width), LOW),
        pltpu.SemaphoreType.DMA((COPIES,)),
        pltpu.SemaphoreType.DMA((COPIES,)),
    ]


class Swap:
    def __init__(self, count, scratch):
        self.count = count
        self.src, self.dst, self.flat, self.send, self.recv = scratch
        self.me = lax.axis_index("dp")
        self.each = self.flat.shape[0] // count
        self.whole = self.each % 16 == 0

    def others(self):
        return [{"dp": lax.rem(self.me + shift, self.count)} for shift in range(1, self.count)]

    def spot(self, ref, index):
        if self.whole:
            return ref.at[pl.ds(pl.multiple_of(index * self.each, 16), self.each)]
        return ref.at[index]

    def copy(self, shift, source, target):
        return remote(
            self.spot(self.src, target), self.spot(self.dst, source),
            self.send.at[shift], self.recv.at[shift], {"dp": target},
        )

    def start(self, values):
        if self.whole:
            self.src[...] = values
        else:
            for index in range(self.count):
                self.src[index] = values[index * self.each : (index + 1) * self.each].astype(FULL)
        order = sorted(range(1, self.count), key=lambda shift: -min(shift, self.count - shift))
        for shift in order:
            self.copy(shift, self.me, lax.rem(self.me + shift, self.count)).start()
        if self.whole:
            rows = pl.ds(pl.multiple_of(self.me * self.each, 16), self.each)
            self.dst[rows] = self.src[rows]
        else:
            self.dst[self.me] = self.src[self.me]

    def arrive(self):
        for shift in range(1, self.count):
            source = lax.rem(self.me + self.count - shift, self.count)
            self.copy(shift, source, source).wait_recv()
        if self.whole:
            return self.dst[...].astype(FULL)
        for index in range(self.count):
            self.flat[index * self.each : (index + 1) * self.each] = self.dst[index]
        return self.flat[...]

    def finish(self):
        for shift in range(1, self.count):
            self.copy(shift, self.me, lax.rem(self.me + shift, self.count)).wait_send()


def swap_scratch(rows, width, count):
    each = rows // count
    block = (rows, width) if each % 16 == 0 else (count, each, width)
    kind = LOW if each % 16 == 0 else FULL
    return [
        pltpu.VMEM(block, kind),
        pltpu.VMEM(block, kind),
        pltpu.VMEM((rows, width), FULL),
        pltpu.SemaphoreType.DMA((count,)),
        pltpu.SemaphoreType.DMA((count,)),
    ]


def placed(slot_ref):
    length = slot_ref.shape[1]
    slots = lax.broadcasted_iota(jnp.int32, (length, length), 0)
    return jnp.where(slots == slot_ref[...], 1.0, 0.0).astype(LOW)


def as_row(ref):
    return ref[...].reshape(1, ref.shape[0])


def pad_into(ref, src):
    ref[...] = jnp.zeros(ref.shape, ref.dtype)
    ref[0 : src.shape[0]] = src[...]


def weight_loads(loads, depth, wqkv, wout, refs):
    wqkv_any, wout_any = refs
    heads = wout_any.shape[1]
    made = [loads.start(wout_any.at[depth], wout.at[pl.ds(0, heads)])]
    for kind in range(3):
        made.append(loads.start(wqkv_any.at[depth, kind], wqkv.at[pl.ds(kind * LANES, heads)]))
    return made


def clear_spare(wqkv, wout, heads):
    width = wout.shape[1]
    wout[heads:LANES] = jnp.zeros((LANES - heads, width), LOW)
    for kind in range(3):
        wqkv[kind * LANES + heads : (kind + 1) * LANES] = jnp.zeros((LANES - heads, width), LOW)


def forward_kernel(
    caption_counts, region_counts,
    features, boxes_ref, w_box_ref, gain_ref, enc_ref, cap_ref, slot_ref,
    b_qv, b_up, row_biases, norm_gains,
    feat_any, wqkv_any, wout_any, wup_any, wdown_any,
    x_out, pre_out, u_out, v_out, ga_out, qkv_out, p_out, ctx_out, hid_out, act_out, slope_out,
    w_feat, wqkv, wout, wup, wdown, biases, boxes, w_box, key_rows,
    ga, qkv, weights, ctx, hid, act, slope, u_buf, v_buf, x_buf, load_sem, save_sem, *scratch, count
):
    group = Group(scratch[:8])
    swap = Swap(count, scratch[8:])
    me = group.me
    heads = wout_any.shape[1]
    loads, saves = Loads(load_sem), Loads(save_sem)
    feat_load = loads.start(feat_any, w_feat)
    for depth in range(LAYERS):
        clear_spare(wqkv.at[depth], wout.at[depth], heads)
    attend_loads, feed_loads = [], []
    for depth in range(LAYERS):
        attend_loads.append(
            weight_loads(loads, depth, wqkv.at[depth], wout.at[depth], (wqkv_any, wout_any))
        )
        feed_loads.append(
            [
                loads.start(wup_any.at[depth], wup.at[depth]),
                loads.start(wdown_any.at[depth], wdown.at[depth]),
            ]
        )
    greet(group.others() + swap.others())

    pad_into(boxes, boxes_ref)
    pad_into(w_box, w_box_ref)
    feat_load.wait()
    pre = dot_nn(features[...], w_feat[...])
    pre += lax.dot_general(
        boxes[...], w_box[...], (((0,), (0,)), ((), ())),
        precision=lax.Precision.HIGHEST, preferred_element_type=FULL,
    )
    pre += enc_ref[0:1]
    hat, _ = normed_rows(pre)
    swap.start((hat * as_row(gain_ref) + enc_ref[1:2]).astype(LOW))
    pre_out[...] = pre
    x_buf[0:CAP] = cap_ref[...].astype(FULL)
    place = placed(slot_ref)
    biases[...] = jnp.zeros(biases.shape, FULL)
    for depth in range(LAYERS):
        biases[depth, 0:1, 0:heads] = b_qv[depth, 0:1]
        biases[depth, 0:1, 2 * LANES : 2 * LANES + heads] = b_qv[depth, 1:2]
    spots = lax.broadcasted_iota(jnp.int32, (8, SEQ), 1)
    for image in range(GROUP):
        seen = jnp.where(
            spots < CAP, spots - caption_counts[image], spots - CAP - region_counts[image]
        )
        key_rows[image] = jnp.where(seen < 0, 0.0, -1e30)
    masks = head_masks()
    scaled = [(one.astype(FULL) * HD ** (-0.5)).astype(LOW) for one in masks]
    x_buf[CAP:] = dot_nn(place, swap.arrive().astype(LOW))

    for depth in range(LAYERS):

        def attend(image):
            rows = image_rows(image)
            low = (dot_nt(ga[depth, rows], wqkv[depth]) + biases[depth, 0:1]).astype(LOW)
            qkv[depth, rows] = low
            queries, keys_low, values_low = (
                low[:, :LANES], low[:, LANES : 2 * LANES], low[:, 2 * LANES :],
            )
            total = jnp.zeros((ROWS, LANES), FULL)
            for head in range(3):
                scores = dot_nt(queries * scaled[head], keys_low) + key_rows[image, 0:1]
                raised = jnp.exp(scores - jnp.max(scores, axis=-1, keepdims=True))
                prob = (raised * (1.0 / jnp.sum(raised, axis=-1, keepdims=True))).astype(LOW)
                weights[depth, image, head] = prob
                total += dot_nn(prob, values_low * masks[head])
            low_ctx = total.astype(LOW)
            ctx[depth, rows] = low_ctx
            return dot_nn(low_ctx, wout[depth])

        def feed(image):
            rows = image_rows(image)
            pre = dot_nn(hid[depth, rows], wup[depth]) + b_up[depth : depth + 1]
            half = 0.5 * (1.0 + lax.erf(pre * 2.0 ** (-0.5)))
            low = (pre * half).astype(LOW)
            act[depth, rows] = low
            slope[depth, rows] = (
                half + pre * jnp.exp(-0.5 * pre * pre) * 0.3989422804014327
            ).astype(LOW)
            return dot_nn(low, wdown[depth])

        states = x_buf[...]
        ga[depth, image_rows(me)] = states.astype(LOW)
        for one in attend_loads[depth]:
            one.wait()
        total = group.exchange(ga.at[depth], attend)
        for src, dst in ((ga, ga_out), (qkv, qkv_out), (weights, p_out), (ctx, ctx_out)):
            saves.start(src.at[depth], dst.at[depth])
        pre_attn = x_buf[...] + total + row_biases[depth, 0:1]
        hat, _ = normed_rows(pre_attn)
        normed = hat * norm_gains[depth, 0:1] + row_biases[depth, 1:2]
        hid[depth, image_rows(me)] = normed.astype(LOW)
        u_buf[depth] = pre_attn
        saves.start(u_buf.at[depth], u_out.at[depth])
        x_buf[...] = normed
        for one in feed_loads[depth]:
            one.wait()
        total = group.exchange(hid.at[depth], feed, late=True)
        for src, dst in ((hid, hid_out), (act, act_out), (slope, slope_out)):
            saves.start(src.at[depth], dst.at[depth])
        pre_ffn = x_buf[...] + total + row_biases[depth, 2:3]
        v_buf[depth] = pre_ffn
        saves.start(v_buf.at[depth], v_out.at[depth])
        hat, _ = normed_rows(pre_ffn)
        x_buf[...] = hat * norm_gains[depth, 1:2] + row_biases[depth, 3:4]

    x_out[...] = x_buf[...]
    swap.finish()
    for depth in range(LAYERS):
        for place, (src, dst) in enumerate(
            (
                (ga, ga_out), (qkv, qkv_out), (weights, p_out), (ctx, ctx_out), (u_buf, u_out),
                (hid, hid_out), (act, act_out), (slope, slope_out), (v_buf, v_out),
            )
        ):
            pltpu.make_async_copy(
                src.at[depth], dst.at[depth], save_sem.at[9 * depth + place]
            ).wait()


def forward(
    count, caption_counts, region_counts, features, boxes, w_box, gain, enc, captions, slots,
    b_qv, b_up, row_biases, norm_gains, w_feat, wqkv, wout, wup, wdown,
):
    width = captions.shape[1]
    hidden = wup.shape[2]
    rows = features.shape[0]
    group = GROUP * ROWS
    saved = [
        ((LAYERS, group, width), LOW),
        ((LAYERS, group, 3 * LANES), LOW),
        ((LAYERS, GROUP, 3, ROWS, ROWS), LOW),
        ((LAYERS, group, LANES), LOW),
        ((LAYERS, group, width), LOW),
        ((LAYERS, group, hidden), LOW),
        ((LAYERS, group, hidden), LOW),
    ]
    kept = ((LAYERS, ROWS, width), FULL)
    shapes = [((ROWS, width), FULL), ((rows, width), FULL), kept, kept] + saved
    vmem = pl.BlockSpec(memory_space=pltpu.VMEM)
    smem = pl.BlockSpec(memory_space=pltpu.SMEM)
    loose = pl.BlockSpec(memory_space=pl.ANY)
    return pl.pallas_call(
        functools.partial(forward_kernel, count=count),
        out_shape=[jax.ShapeDtypeStruct(*one) for one in shapes],
        in_specs=[smem] * 2 + [vmem] * 11 + [loose] * 5,
        out_specs=[vmem] * 2 + [loose] * 9,
        scratch_shapes=[
            pltpu.VMEM(w_feat.shape, LOW),
            pltpu.VMEM((LAYERS, 3 * LANES, width), LOW),
            pltpu.VMEM((LAYERS, LANES, width), LOW),
            pltpu.VMEM(wup.shape, LOW),
            pltpu.VMEM(wdown.shape, LOW),
            pltpu.VMEM((LAYERS, 8, 3 * LANES), FULL),
            pltpu.VMEM((8, rows), FULL),
            pltpu.VMEM((8, width), FULL),
            pltpu.VMEM((GROUP, 8, SEQ), FULL),
        ]
        + [pltpu.VMEM(*one) for one in saved]
        + [pltpu.VMEM(*kept), pltpu.VMEM(*kept), pltpu.VMEM((ROWS, width), FULL)]
        + [pltpu.SemaphoreType.DMA((1 + 6 * LAYERS,)), pltpu.SemaphoreType.DMA((9 * LAYERS,))]
        + group_scratch(width)
        + swap_scratch(rows, width, count),
        compiler_params=pltpu.CompilerParams(
            collective_id=0, has_side_effects=True, vmem_limit_bytes=60 * 2**20
        ),
    )(
        caption_counts, region_counts, features, boxes, w_box, gain, enc, captions, slots,
        b_qv, b_up, row_biases, norm_gains, w_feat, wqkv, wout, wup, wdown,
    )


def ring_places(count):
    me = lax.axis_index("dp")
    half = count // 2

    def device(place):
        side = place // half
        depth = place + side * (count - 1 - 2 * place)
        return 2 * depth + side

    side = lax.rem(me, 2)
    depth = me // 2
    place = depth + side * (count - 1 - 2 * depth)
    return place, device(lax.rem(place + 1, count)), device(lax.rem(place + count - 1, count))


def ring_rows(length, count):
    each = -(-length // (16 * count))
    first = 16 * (each // 2)
    sizes = (first, 16 * each - first) if first else (16 * each,)
    return count * each * 16, sizes


class Ring:
    def __init__(self, count, places, pack, lands, sems, passed=None, flush=None):
        self.count, self.last = count, count - 1
        self.place, self.after, self.before = places
        self.pack, self.lands, self.sems = pack, lands, sems
        self.sizes = [land.shape[1] for land in lands]
        self.ways = range(len(self.sizes))
        self.taken, self.due = 0, 0
        self.passed, self.flush = passed, flush

    def chunk(self, way, offset):
        spot = lax.rem(self.place + (offset if way else -offset) + 2 * self.count, self.count)
        start = spot * sum(self.sizes) + way * self.sizes[0]
        return pl.ds(pl.multiple_of(start, 16), self.sizes[way])

    def copy(self, phase, way, step, rows=None):
        if phase == 0:
            src = self.pack.at[self.chunk(way, 0)] if step == 0 else self.lands[way].at[step - 1]
            dst = self.lands[way].at[step]
        else:
            if rows is None:
                rows = self.chunk(way, step - 1)
            src = self.pack.at[rows]
            dst = self.pack.at[rows]
        return remote(
            src, dst, self.sems.at[2 * phase, way, step], self.sems.at[2 * phase + 1, way, step],
            {"dp": self.before if way else self.after},
        )

    def running(self):
        return self.taken <= 2 * self.last

    def step(self):
        index, last = self.taken, self.last
        for way in self.ways:
            if index == 0:
                self.copy(0, way, 0).start()
            elif index <= last:
                done = index - 1
                self.copy(0, way, done).wait_recv()
                if done == 0:
                    self.copy(0, way, 0).wait_send()
                rows = self.chunk(way, done + 1)
                added = (self.lands[way][done].astype(FULL) + self.pack[rows].astype(FULL)).astype(LOW)
                if index < last:
                    self.lands[way][done] = added
                    self.copy(0, way, index).start()
                else:
                    self.pack[rows] = added
                    self.copy(1, way, 0).start()
                    self.pass_on(rows)
            else:
                done = index - last - 1
                rows = self.chunk(way, done)
                self.copy(1, way, done, rows).wait_recv()
                if done + 1 < last:
                    self.copy(1, way, done + 1).start()
                self.pass_on(rows)
        self.taken += 1
        if not self.running() and self.flush is not None:
            self.flush()

    def pass_on(self, rows):
        if self.passed is not None:
            self.passed(rows)

    def finish(self):
        for phase in range(2):
            for way in self.ways:
                for step in range(1 - phase, self.last):
                    self.copy(phase, way, step).wait_send()


class Clock:
    def __init__(self):
        self.now, self.link, self.rings = 0, 0, []

    def add(self, ring):
        ring.due = self.now
        self.rings.append(ring)

    def running(self):
        return [ring for ring in self.rings if ring.running()]

    def visit(self, ring):
        self.now = max(self.now, ring.due)
        ring.step()
        self.link = max(self.link, self.now) + max(ring.sizes) * 0.036
        ring.due = self.link + 2

    def tick(self, weight):
        self.now += weight
        for ring in sorted(self.running(), key=lambda one: one.due):
            if ring.due <= self.now:
                self.visit(ring)

    def drain(self, first):
        while self.running():
            self.visit(
                min(
                    self.running(),
                    key=lambda one: one.due + 1.5 * one.taken - (3 if one is first else 0),
                )
            )


def backward_kernel(
    cot_ref, slot_ref, boxes_ref, gain_ref, pre_ref, norm_gains,
    wqkv_any, wout_any, wup_any, wdown_any, u_any, v_any,
    ga_any, qkv_any, p_any, ctx_any, hid_any, act_any, slope_any, feat_any, w_feat_any,
    cap_out, back_out, box_out, gain_out, enc_out, qv_out, up_sum_out, norms_out, rows_out,
    down_out, up_out, out_out, mixed_out, feat_out,
    wqkv, wout, wup, wdown, u_buf, v_buf,
    ga, qkv, weights, ctx, hid, act, slope, low_e, d_up, low_f, d_mixed,
    keep, small, small_in, extra_sum, extra_in, down_pack, up_pack, thin_pack, ring_sems,
    features, boxes, feat_in, feat_send, feat_pack, feat_sems,
    send, recv, small_send, small_recv, load_sem, local_sem, *scratch, count, ways
):
    group = Group(scratch[:8])
    swap = Swap(count, scratch[8:13])
    lands = list(scratch[13:])
    down_lands, up_lands, thin_lands, feat_lands = (
        [lands.pop(0) for _ in range(number)] for number in ways
    )
    me, mate, peer, diag = group.me, group.mate, group.peer, group.diag
    width = keep.shape[1]
    heads = wout_any.shape[1]
    hidden = act.shape[1]
    loads, local = Loads(load_sem), Loads(local_sem)

    def feed_load(depth):
        return [
            loads.start(src.at[depth], dst)
            for src, dst in (
                (v_any, v_buf), (wdown_any, wdown), (slope_any, slope), (wup_any, wup),
                (act_any, act), (hid_any, hid),
            )
        ]

    def attend_load(depth):
        return [
            loads.start(src.at[depth], dst)
            for src, dst in (
                (u_any, u_buf), (p_any, weights), (qkv_any, qkv), (ctx_any, ctx), (ga_any, ga),
            )
        ] + weight_loads(loads, depth, wqkv, wout, (wqkv_any, wout_any))

    feed_waits = feed_load(LAYERS - 1)
    clear_spare(wqkv, wout, heads)
    attend_waits = attend_load(LAYERS - 1)
    greet(group.others() + swap.others())
    places = ring_places(count)

    def down_flush(depth):
        local.start(down_pack.at[depth, pl.ds(0, hidden)], down_out.at[depth])

    def up_flush(depth):
        local.start(up_pack.at[depth, pl.ds(0, width)], up_out.at[depth])

    def thin_flush(depth):
        local.start(thin_pack.at[depth, pl.ds(0, heads)], out_out.at[depth])
        for kind in range(3):
            rows = pl.ds(heads * (kind + 1), heads)
            local.start(thin_pack.at[depth, rows], mixed_out.at[depth, kind])

    def rings(spot, pack, own_lands, flush):
        return [
            Ring(
                count, places, pack.at[depth], [one.at[depth] for one in own_lands],
                ring_sems.at[spot, depth], flush=functools.partial(flush, depth),
            )
            for depth in range(LAYERS)
        ]

    downs = rings(0, down_pack, down_lands, down_flush)
    ups = rings(1, up_pack, up_lands, up_flush)
    thins = rings(2, thin_pack, thin_lands, thin_flush)
    clock = Clock()
    tick = clock.tick
    masks = head_masks()

    for depth in reversed(range(LAYERS)):

        def feed_back(image):
            rows = image_rows(image)
            low = (dot_nt(low_e[rows], wdown[...]) * slope[rows].astype(FULL)).astype(LOW)
            d_up[rows] = low
            tick(0.8)
            return dot_nt(low, wup[...])

        def attend_back(image):
            rows = image_rows(image)
            d_ctx = dot_nt(low_f[rows], wout[...]).astype(LOW)
            low = qkv[rows]
            queries, keys_low, values_low = (
                low[:, :LANES], low[:, LANES : 2 * LANES], low[:, 2 * LANES :],
            )
            d_q = jnp.zeros((ROWS, LANES), FULL)
            d_k = jnp.zeros((ROWS, LANES), FULL)
            d_v = jnp.zeros((ROWS, LANES), FULL)
            for head in range(3):
                own = d_ctx * masks[head]
                prob_low = weights[image, head]
                d_v += dot_tn(prob_low, own)
                d_prob = dot_nt(own, values_low)
                prob = prob_low.astype(FULL)
                meant = jnp.sum(prob * d_prob, axis=-1, keepdims=True)
                d_score = (prob * (d_prob - meant)).astype(LOW)
                d_q += dot_nn(d_score, keys_low * masks[head])
                d_k += dot_tn(d_score, queries * masks[head])
                tick(1.2)
            scaling = HD ** (-0.5)
            d_mixed[rows, 0:LANES] = (d_q * scaling).astype(LOW)
            d_mixed[rows, LANES : 2 * LANES] = (d_k * scaling).astype(LOW)
            d_mixed[rows, 2 * LANES : 3 * LANES] = d_v.astype(LOW)
            return dot_nn(d_mixed[rows], wqkv[...])

        def down_fill(start):
            def fill():
                down_pack[depth, start : start + LANES] = dot_tn(
                    act[:, start : start + LANES], low_e[...]
                ).astype(LOW)

            return fill

        def up_fill(start):
            def fill():
                up_pack[depth, start : start + LANES] = dot_tn(
                    hid[:, start : start + LANES], d_up[...]
                ).astype(LOW)

            return fill

        def out_fill():
            thin_pack[depth, 0:heads] = dot_tn(ctx[...], low_f[...])[:heads].astype(LOW)

        def mixed_fill(kind):
            def fill():
                base = heads * (kind + 1)
                made = dot_tn(d_mixed[:, kind * LANES : (kind + 1) * LANES], ga[...])
                thin_pack[depth, base : base + heads] = made[:heads].astype(LOW)

            return fill

        def small_copy(spot, target):
            return remote(
                small.at[depth], small_in.at[depth, spot],
                small_send.at[depth, spot], small_recv.at[depth, spot], {"mp": target},
            )

        first, second = small_copy(0, mate), small_copy(1, peer)

        def small_fill():
            first.wait_recv()
            first.wait_send()
            small[depth] += small_in[depth, 0]
            second.start()

        gradient = cot_ref[...].astype(FULL) if depth == LAYERS - 1 else keep[...]
        feed_waits[0].wait()
        d_pre, hat = normed_back(gradient, v_buf[...], norm_gains[depth, 1:2])
        low_e[image_rows(me)] = d_pre.astype(LOW)
        keep[...] = d_pre
        small[depth] = jnp.zeros((8, width), FULL)
        small[depth, 1:2] = row_sum(gradient * hat)
        small[depth, 4:5] = row_sum(d_pre)
        small[depth, 5:6] = row_sum(gradient)
        for one in feed_waits[1:]:
            one.wait()
        total = group.exchange(
            low_e, feed_back, tick,
            [down_fill(start) for start in range(0, hidden, LANES)]
            + [functools.partial(clock.add, downs[depth])]
            + [up_fill(start) for start in range(0, width, LANES)]
            + [functools.partial(clock.add, ups[depth])],
        )
        tick(2)
        b_up_sum = row_sum(d_up[...].astype(FULL))
        if depth:
            feed_waits = feed_load(depth - 1)
        gradient = keep[...] + total
        if depth < LAYERS - 1:
            pass
        attend_waits[0].wait()
        d_pre, hat = normed_back(gradient, u_buf[...], norm_gains[depth, 0:1])
        low_f[image_rows(me)] = d_pre.astype(LOW)
        keep[...] = d_pre
        small[depth, 0:1] = row_sum(gradient * hat)
        small[depth, 2:3] = row_sum(d_pre)
        small[depth, 3:4] = row_sum(gradient)
        first.start()
        for one in attend_waits[1:]:
            one.wait()
        total = group.exchange(
            low_f, attend_back, tick,
            [small_fill, out_fill]
            + [mixed_fill(kind) for kind in range(3)]
            + [functools.partial(clock.add, thins[depth])],
            late=True,
        )
        tick(2)
        second.wait_recv()
        second.wait_send()
        small[depth] += small_in[depth, 1]
        small[depth, 6:7] = b_up_sum
        small[depth, 7:8] = row_sum(d_mixed[...].astype(FULL))
        if depth:
            attend_waits = attend_load(depth - 1)
        keep[...] += total

    cap_out[...] = keep[0:CAP]
    place = placed(slot_ref)
    swap.start(dot_tn(place, keep[CAP:].astype(LOW)).astype(LOW))
    span = act.shape[0]
    feat_loads = [
        loads.start(feat_any, features),
        loads.start(w_feat_any.at[pl.ds(0, span)], act),
        loads.start(w_feat_any.at[pl.ds(span, span)], slope),
    ]
    pad_into(boxes, boxes_ref)
    each = feat_send.shape[0]
    gradient = swap.arrive()
    tick(6)
    d_pre, hat = normed_back(gradient, pre_ref[...], as_row(gain_ref))
    low = d_pre.astype(LOW)
    feat_loads[0].wait()

    def product(ref, spot):
        columns = pl.ds(pl.multiple_of(spot * each, 128), each)
        ref[0:each] = dot_tn(features[:, columns], low).astype(LOW)

    def copy(src, dst, spot, target):
        return remote(src, dst, send.at[spot], recv.at[spot], {"mp": target})

    span_rows = pl.ds(0, each)
    to_mate = [
        copy(low_e.at[span_rows], feat_in.at[0], 0, mate),
        copy(d_up.at[span_rows], feat_in.at[1], 1, mate),
    ]
    product(low_e, diag)
    to_mate[0].start()
    product(low_f, peer)
    tick(1.5)
    to_mate[0].wait_recv()
    feat_send[...] = (low_f[0:each].astype(FULL) + feat_in[0].astype(FULL)).astype(LOW)
    to_peer = copy(feat_send, feat_in.at[2], 2, peer)
    to_peer.start()
    tick(2)
    rounded = low.astype(FULL)
    extra_sum[...] = jnp.concatenate(
        [
            lax.dot_general(
                boxes[...], rounded, (((1,), (0,)), ((), ())),
                precision=lax.Precision.HIGHEST, preferred_element_type=FULL,
            ),
            row_sum(gradient * hat),
            row_sum(rounded),
            row_sum(gradient),
            jnp.zeros((5, width), FULL),
        ],
        axis=0,
    )
    extras = [copy(extra_sum, extra_in.at[spot], 6 + spot, target) for spot, target in ((0, mate), (1, peer))]
    extras[0].start()
    product(d_up, mate)
    to_mate[1].start()
    tick(1)
    product(hid, me)
    tick(1)
    extras[0].wait_recv()
    extras[0].wait_send()
    extra_sum[...] += extra_in[0]
    extras[1].start()
    feat_loads[1].wait()
    back_out[:, 0:span] = dot_nt(low, act[...])
    tick(1)
    feat_loads[2].wait()
    back_out[:, span:] = dot_nt(low, slope[...])
    to_mate[1].wait_recv()
    own = hid[0:each].astype(FULL) + feat_in[1].astype(FULL)
    hid[0:each] = own.astype(LOW)
    tick(1.5)
    extras[1].wait_recv()
    extras[1].wait_send()
    base = each + 16
    feat_pack[each:base] = (extra_sum[...] + extra_in[1]).astype(LOW)
    for depth in range(LAYERS):
        feat_pack[base : base + 16] = jnp.concatenate(
            [small[depth], jnp.zeros((8, width), FULL)], axis=0
        ).astype(LOW)
        base += 16
    feat_rows = feat_pack.shape[0]
    if feat_rows > base:
        feat_pack[base:] = jnp.zeros((feat_rows - base, width), LOW)
    for _ in range(6):
        tick(2)
    to_peer.wait_recv()
    feat_pack[0:each] = (hid[0:each].astype(FULL) + feat_in[2].astype(FULL)).astype(LOW)

    def ours(spot, start, size):
        return feat_out.at[pl.ds(pl.multiple_of(spot * each + start, 16), size)]

    def spread(rows):
        @pl.when(rows.start < each)
        def _():
            for spot, target in ((3, peer), (4, mate)):
                copy(feat_pack.at[rows], ours(me, rows.start, rows.size), spot, target).start()

    feat = Ring(count, places, feat_pack, feat_lands, feat_sems, spread)
    clock.add(feat)
    clock.drain(feat)
    local.start(feat_pack.at[span_rows], ours(me, 0, each))
    base = each
    box_out[...] = feat_pack[base : base + 16].astype(FULL)[0:4]
    gain_out[...] = feat_pack[base : base + 16].astype(FULL)[8:9]
    enc_out[...] = feat_pack[base : base + 16].astype(FULL)[9:11]
    for depth in range(LAYERS):
        base += 16
        sums = feat_pack[base : base + 16].astype(FULL)
        norms_out[depth] = sums[0:2]
        rows_out[depth] = sums[2:6]
        up_sum_out[depth : depth + 1] = sums[6:7]
        qv_out[depth, 0:1] = sums[7:8, 0:heads]
        qv_out[depth, 1:2] = sums[7:8, 2 * LANES : 2 * LANES + heads]
    copy(feat_send, ours(peer, 0, each), 3, peer).wait_recv()
    relay = copy(ours(peer, 0, each), ours(peer, 0, each), 5, mate)
    relay.start()
    copy(feat_send, ours(mate, 0, each), 4, mate).wait_recv()
    copy(feat_send, ours(diag, 0, each), 5, mate).wait_recv()
    for spot in (3, 4):
        copy(feat_send, ours(me, 0, each), spot, mate).wait_send()
    for one in to_mate + [to_peer, relay]:
        one.wait_send()
    for ring in downs + ups + thins + [feat]:
        ring.finish()
    swap.finish()
    for one in local.made:
        one.wait()


def backward(
    count, cotangent, slots, boxes, gain, pre, norm_gains, wqkv, wout, wup, wdown, kept,
    features, w_feat,
):
    width = cotangent.shape[1]
    rows, columns = features.shape
    hidden = wup.shape[2]
    heads = wout.shape[1]
    group = GROUP * ROWS
    each = columns // GROUP
    down_rows, down_sizes = ring_rows(hidden, count)
    up_rows, up_sizes = ring_rows(width, count)
    thin_rows, thin_sizes = ring_rows(GROUP * heads, count)
    feat_rows, feat_sizes = ring_rows(each + 16 + 16 * LAYERS, count)

    def ring_sems(*lead):
        return pltpu.SemaphoreType.DMA(lead + (4, 2, count - 1))

    vmem = pl.BlockSpec(memory_space=pltpu.VMEM)
    loose = pl.BlockSpec(memory_space=pl.ANY)
    packs = [((LAYERS, size, width), LOW) for size in (down_rows, up_rows, thin_rows)]
    shapes = [
        ((CAP, width), FULL),
        ((rows, columns), FULL),
        ((4, width), FULL),
        ((1, width), FULL),
        ((2, width), FULL),
        ((LAYERS, 2, heads), FULL),
        ((LAYERS, hidden), FULL),
        ((LAYERS, 2, width), FULL),
        ((LAYERS, 4, width), FULL),
        ((LAYERS, hidden, width), LOW),
        ((LAYERS, width, hidden), LOW),
        ((LAYERS, heads, width), LOW),
        ((LAYERS, 3, heads, width), LOW),
        ((columns, width), LOW),
    ]
    return pl.pallas_call(
        functools.partial(
            backward_kernel,
            count=count,
            ways=[len(one) for one in (down_sizes, up_sizes, thin_sizes, feat_sizes)],
        ),
        out_shape=[jax.ShapeDtypeStruct(*one) for one in shapes],
        in_specs=[vmem] * 6 + [loose] * 15,
        out_specs=[vmem] * 9 + [loose] * 5,
        scratch_shapes=[
            pltpu.VMEM((3 * LANES, width), LOW),
            pltpu.VMEM((LANES, width), LOW),
            pltpu.VMEM(wup.shape[1:], LOW),
            pltpu.VMEM(wdown.shape[1:], LOW),
            pltpu.VMEM((ROWS, width), FULL),
            pltpu.VMEM((ROWS, width), FULL),
        ]
        + [pltpu.VMEM(one.shape[1:], one.dtype) for one in kept[2:]]
        + [
            pltpu.VMEM((group, width), LOW),
            pltpu.VMEM((group, hidden), LOW),
            pltpu.VMEM((group, width), LOW),
            pltpu.VMEM((group, 3 * LANES), LOW),
            pltpu.VMEM((ROWS, width), FULL),
            pltpu.VMEM((LAYERS, 8, width), FULL),
            pltpu.VMEM((LAYERS, 2, 8, width), FULL),
            pltpu.VMEM((16, width), FULL),
            pltpu.VMEM((2, 16, width), FULL),
        ]
        + [pltpu.VMEM(*one) for one in packs]
        + [ring_sems(3, LAYERS)]
        + [
            pltpu.VMEM(features.shape, LOW),
            pltpu.VMEM((8, rows), FULL),
            pltpu.VMEM((3, each, width), LOW),
            pltpu.VMEM((each, width), LOW),
            pltpu.VMEM((feat_rows, width), LOW),
            ring_sems(),
            pltpu.SemaphoreType.DMA((8,)),
            pltpu.SemaphoreType.DMA((8,)),
            pltpu.SemaphoreType.DMA((LAYERS, 2)),
            pltpu.SemaphoreType.DMA((LAYERS, 2)),
            pltpu.SemaphoreType.DMA((15 * LAYERS + 3,)),
            pltpu.SemaphoreType.DMA((1 + 6 * LAYERS,)),
        ]
        + group_scratch(width)
        + swap_scratch(rows, width, count)
        + [
            pltpu.VMEM((LAYERS, count - 1, size, width), LOW) for size in down_sizes + up_sizes + thin_sizes
        ]
        + [pltpu.VMEM((count - 1, size, width), LOW) for size in feat_sizes],
        compiler_params=pltpu.CompilerParams(
            collective_id=1, has_side_effects=True, vmem_limit_bytes=62 * 2**20
        ),
    )(
        cotangent, slots, boxes, gain, pre, norm_gains, wqkv, wout, wup, wdown, *kept,
        features, w_feat,
    )


def finish_kernel(*refs):
    half = len(refs) // 2
    for src, dst in zip(refs[:half], refs[half:]):
        values = src[...].astype(FULL)
        dst[...] = values.reshape(dst.shape) if len(dst.shape) == 1 else values


def finish(tall, small, shapes):
    blocks = 8
    tall = [one.reshape(-1, one.shape[-1]) for one in tall]
    specs = [
        pl.BlockSpec((one.shape[0] // blocks, one.shape[1]), lambda step: (step, 0)) for one in tall
    ]
    whole = [pl.BlockSpec(memory_space=pltpu.VMEM)] * len(small)
    made = pl.pallas_call(
        finish_kernel,
        grid=(blocks,),
        out_shape=[jax.ShapeDtypeStruct(one.shape, FULL) for one in tall]
        + [jax.ShapeDtypeStruct(one, FULL) for one in shapes],
        in_specs=specs + whole,
        out_specs=specs + whole,
        compiler_params=pltpu.CompilerParams(vmem_limit_bytes=40 * 2**20),
    )(*tall, *small)
    return made[: len(tall)], made[len(tall) :]


def on_device(
    captions,
    features,
    region_boxes,
    caption_counts,
    region_counts,
    slot_map,
    w_feat,
    w_box,
    enc_gain,
    enc_vectors,
    w_qkv,
    b_qv,
    w_out,
    w_up,
    b_up,
    w_down,
    norm_gains,
    row_biases,
    cotangent,
):
    count = lax.axis_size("dp")
    wqkv = w_qkv.transpose(0, 2, 3, 1)
    layer_output, enc_pre, *kept = forward(
        count, caption_counts, region_counts, features, region_boxes, w_box, enc_gain, enc_vectors,
        captions, slot_map, b_qv, b_up, row_biases, norm_gains, w_feat, wqkv, w_out, w_up, w_down,
    )
    (
        caption_grad, feature_grad, box_sum, gain_sum, enc_sum, qv_sum, up_sum, norm_sum, row_sums,
        down, up, out, mixed, feat,
    ) = backward(
        count, cotangent, slot_map, region_boxes, enc_gain, enc_pre, norm_gains, wqkv, w_out, w_up,
        w_down, kept, features, w_feat,
    )
    tall, sums = finish(
        [layer_output, caption_grad, feature_grad, feat, mixed, out, up, down],
        [box_sum, gain_sum, enc_sum, qv_sum, up_sum, norm_sum, row_sums],
        [box_sum.shape, enc_gain.shape] + [one.shape for one in (enc_sum, qv_sum, up_sum, norm_sum, row_sums)],
    )
    layer_output, caption_grad, feature_grad, feat, mixed_grad, out_grad, up_grad, down_grad = tall
    box_sum, gain_sum, enc_sum, qv_sum, up_sum, norm_sum, row_sums = sums
    return (
        layer_output,
        caption_grad,
        feature_grad,
        feat,
        box_sum,
        gain_sum,
        enc_sum,
        mixed_grad.reshape(mixed.shape).transpose(0, 3, 1, 2),
        qv_sum,
        out_grad.reshape(out.shape),
        up_grad.reshape(up.shape),
        up_sum,
        down_grad.reshape(down.shape),
        norm_sum,
        row_sums,
    )


def solution(mesh):
    return jax.shard_map(
        on_device,
        mesh=mesh,
        in_specs=(
            P(("dp", "mp"), None),
            P(("dp", "mp"), None),
            P(None, ("dp", "mp")),
            P("dp"),
            P("dp"),
            P(("dp", "mp"), None),
            P(),
            P(),
            P(),
            P(),
            P(None, None, None, "mp"),
            P(None, None, "mp"),
            P(None, "mp", None),
            P(None, None, "mp"),
            P(None, "mp"),
            P(None, "mp", None),
            P(),
            P(),
            P(("dp", "mp"), None),
        ),
        out_specs=(
            P(("dp", "mp"), None),
            P(("dp", "mp"), None),
            P(("dp", "mp"), None),
            P(),
            P(),
            P(),
            P(),
            P(None, None, None, "mp"),
            P(None, None, "mp"),
            P(None, "mp", None),
            P(None, None, "mp"),
            P(None, "mp"),
            P(None, "mp", None),
            P(),
            P(),
        ),
        check_vma=False,
    )
```

```python
import functools

import jax
import jax.numpy as jnp
from jax import lax
from jax.experimental import pallas as pl
from jax.experimental.pallas import tpu as pltpu
from jax.sharding import PartitionSpec as P

HD = 64
CAP = 128
RPAD = 128
LAYERS = 2
SEQ = 256
ROWS = SEQ
HALF = ROWS // 2
LANES = 256
GROUP = 4
COPIES = 10
LOW, FULL = jnp.bfloat16, jnp.float32
MESH = pl.DeviceIdType.MESH

epsilon = 1e-05


def dot_nn(left, right):
    return jnp.dot(left, right, preferred_element_type=FULL)


def dot_nt(left, right):
    return lax.dot_general(left, right, (((1,), (1,)), ((), ())), preferred_element_type=FULL)


def dot_tn(left, right):
    return lax.dot_general(left, right, (((0,), (0,)), ((), ())), preferred_element_type=FULL)


def row_sum(values):
    return jnp.sum(values, axis=0, keepdims=True)


def normed_rows(values):
    centre = values - jnp.mean(values, axis=-1, keepdims=True)
    spread = jnp.mean(centre * centre, axis=-1, keepdims=True)
    inverse = lax.rsqrt(spread + epsilon)
    return centre * inverse, inverse


def normed_back(gradient, values, gain):
    hat, inverse = normed_rows(values)
    scaled = gradient * gain
    tilt = jnp.mean(scaled * hat, axis=-1, keepdims=True)
    level = jnp.mean(scaled, axis=-1, keepdims=True)
    return inverse * (scaled - level - hat * tilt), hat


def head_masks():
    lane = lax.broadcasted_iota(jnp.int32, (1, LANES), 1)
    return [
        jnp.where((lane >= head * HD) & (lane < head * HD + HD), 1.0, 0.0).astype(LOW)
        for head in range(3)
    ]


def image_rows(image):
    return pl.ds(pl.multiple_of(image * ROWS, ROWS), ROWS)


def half_rows(half, image=0):
    return pl.ds(pl.multiple_of(image * ROWS + half * HALF, HALF), HALF)


def remote(src, dst, send_sem, recv_sem, target):
    return pltpu.make_async_remote_copy(
        src_ref=src,
        dst_ref=dst,
        send_sem=send_sem,
        recv_sem=recv_sem,
        device_id=target,
        device_id_type=MESH,
    )


def greet(targets):
    barrier = pltpu.get_barrier_semaphore()
    for target in targets:
        pl.semaphore_signal(barrier, inc=1, device_id=target, device_id_type=MESH)
    pl.semaphore_wait(barrier, len(targets))


class Loads:
    def __init__(self, sems):
        self.sems, self.used, self.made = sems, 0, []

    def start(self, src, dst):
        one = pltpu.make_async_copy(src, dst, self.sems.at[self.used])
        self.used += 1
        self.made.append(one)
        one.start()
        return one


class Group:
    def __init__(self, scratch):
        self.me = lax.axis_index("mp")
        self.core = lax.rem(self.me, 2)
        self.mate = self.me + 1 - 2 * self.core
        self.peer = lax.rem(self.me + 2, GROUP)
        self.diag = lax.rem(self.mate + 2, GROUP)
        self.near = self.me - self.core
        self.far = self.peer - self.core
        (
            self.acc, self.far_acc, self.near_sums, self.mixed_sums, self.far_sums, self.out_sums,
            self.send, self.recv,
        ) = scratch

    def others(self):
        return [{"mp": one} for one in (self.mate, self.peer, self.diag)]

    def copy(self, src, dst, spot, target, arrival=None):
        arrival = spot if arrival is None else arrival
        return remote(src, dst, self.send.at[spot], self.recv.at[arrival], {"mp": target})

    def exchange(self, gath, part, tick=lambda weight: None, fills=(), late=False):
        core, mate, other = self.core, self.mate, 1 - self.core

        def same(rows, spot, target):
            return self.copy(gath.at[rows], gath.at[rows], spot, target)

        def relayed(which):
            rows = half_rows(core, self.far + which)
            same(rows, 1 + which, self.peer).wait_recv()
            one = same(rows, 3 + which, mate)
            one.start()
            sent.append(one)

        sent = [same(image_rows(self.me), 0, mate)]
        sent[0].start()
        across = [
            same(half_rows(core, self.near + which), 1 + which, self.peer) for which in (0, 1)
        ]
        pl.when(core == 0)(across[0].start)
        same(image_rows(mate), 0, mate).wait_recv()
        pl.when(core == 1)(across[0].start)
        across[1].start()
        sent += across
        tick(2)
        self.acc[...] = part(self.me)
        tick(0.4)
        relayed(0)
        near = self.copy(self.near_sums.at[0], self.near_sums.at[1], 5, mate)

        def near_part():
            self.near_sums[0] = part(mate).astype(LOW)
            near.start()
            sent.append(near)
            tick(0.4)

        if not late:
            near_part()
        for which in (0, 1):
            image = self.far + which
            same(half_rows(other, image), 3 + which, mate).wait_recv()
            tick(1.5)
            self.far_acc[...] = part(image)
            self.mixed_sums[2 * which] = self.far_acc[half_rows(other)].astype(LOW)
            mixed = self.copy(
                self.mixed_sums.at[2 * which], self.mixed_sums.at[2 * which + 1], 6 + which, mate
            )
            mixed.start()
            if which == 0:
                relayed(1)
            tick(0.4)
            mixed.wait_recv()
            self.out_sums[which] = (
                self.far_acc[half_rows(core)] + self.mixed_sums[2 * which + 1].astype(FULL)
            ).astype(LOW)
            out = self.copy(
                self.out_sums.at[which], self.far_sums.at[half_rows(core)], 8 + which, image, 8 + core
            )
            out.start()
            sent += [mixed, out]
            tick(1.3)
        if late:
            near_part()
        for fill in fills:
            fill()
            tick(0.6)
        near.wait_recv()
        self.acc[...] += self.near_sums[1].astype(FULL)
        for half in (0, 1):
            self.copy(
                self.out_sums.at[0], self.far_sums.at[half_rows(half)], 8, self.peer, 8 + half
            ).wait_recv()
        for one in sent:
            one.wait_send()
        return self.acc[...] + self.far_sums[...].astype(FULL)


def group_scratch(width):
    return [
        pltpu.VMEM((ROWS, width), FULL),
        pltpu.VMEM((ROWS, width), FULL),
        pltpu.VMEM((2, ROWS, width), LOW),
        pltpu.VMEM((4, HALF, width), LOW),
        pltpu.VMEM((ROWS, width), LOW),
        pltpu.VMEM((2, HALF, width), LOW),
        pltpu.SemaphoreType.DMA((COPIES,)),
        pltpu.SemaphoreType.DMA((COPIES,)),
    ]


class Swap:
    def __init__(self, count, scratch):
        self.count = count
        self.src, self.dst, self.flat, self.send, self.recv = scratch
        self.me = lax.axis_index("dp")
        self.each = self.flat.shape[0] // count
        self.whole = self.each % 16 == 0

    def others(self):
        return [{"dp": lax.rem(self.me + shift, self.count)} for shift in range(1, self.count)]

    def spot(self, ref, index):
        if self.whole:
            return ref.at[pl.ds(pl.multiple_of(index * self.each, 16), self.each)]
        return ref.at[index]

    def copy(self, shift, source, target):
        return remote(
            self.spot(self.src, target), self.spot(self.dst, source),
            self.send.at[shift], self.recv.at[shift], {"dp": target},
        )

    def start(self, values):
        if self.whole:
            self.src[...] = values
        else:
            for index in range(self.count):
                self.src[index] = values[index * self.each : (index + 1) * self.each].astype(FULL)
        order = sorted(range(1, self.count), key=lambda shift: -min(shift, self.count - shift))
        for shift in order:
            self.copy(shift, self.me, lax.rem(self.me + shift, self.count)).start()
        if self.whole:
            rows = pl.ds(pl.multiple_of(self.me * self.each, 16), self.each)
            self.dst[rows] = self.src[rows]
        else:
            self.dst[self.me] = self.src[self.me]

    def arrive(self):
        for shift in range(1, self.count):
            source = lax.rem(self.me + self.count - shift, self.count)
            self.copy(shift, source, source).wait_recv()
        if self.whole:
            return self.dst[...].astype(FULL)
        for index in range(self.count):
            self.flat[index * self.each : (index + 1) * self.each] = self.dst[index]
        return self.flat[...]

    def finish(self):
        for shift in range(1, self.count):
            self.copy(shift, self.me, lax.rem(self.me + shift, self.count)).wait_send()


def swap_scratch(rows, width, count):
    each = rows // count
    block = (rows, width) if each % 16 == 0 else (count, each, width)
    kind = LOW if each % 16 == 0 else FULL
    return [
        pltpu.VMEM(block, kind),
        pltpu.VMEM(block, kind),
        pltpu.VMEM((rows, width), FULL),
        pltpu.SemaphoreType.DMA((count,)),
        pltpu.SemaphoreType.DMA((count,)),
    ]


def placed(slot_ref):
    length = slot_ref.shape[1]
    slots = lax.broadcasted_iota(jnp.int32, (length, length), 0)
    return jnp.where(slots == slot_ref[...], 1.0, 0.0).astype(LOW)


def as_row(ref):
    return ref[...].reshape(1, ref.shape[0])


def pad_into(ref, src):
    ref[...] = jnp.zeros(ref.shape, ref.dtype)
    ref[0 : src.shape[0]] = src[...]


def weight_loads(loads, depth, wqkv, wout, refs):
    wqkv_any, wout_any = refs
    heads = wout_any.shape[1]
    made = [loads.start(wout_any.at[depth], wout.at[pl.ds(0, heads)])]
    for kind in range(3):
        made.append(loads.start(wqkv_any.at[depth, kind], wqkv.at[pl.ds(kind * LANES, heads)]))
    return made


def clear_spare(wqkv, wout, heads):
    width = wout.shape[1]
    wout[heads:LANES] = jnp.zeros((LANES - heads, width), LOW)
    for kind in range(3):
        wqkv[kind * LANES + heads : (kind + 1) * LANES] = jnp.zeros((LANES - heads, width), LOW)


def forward_kernel(
    caption_counts, region_counts,
    features, boxes_ref, w_box_ref, gain_ref, enc_ref, cap_ref, slot_ref,
    b_qv, b_up, row_biases, norm_gains,
    feat_any, wqkv_any, wout_any, wup_any, wdown_any,
    x_out, pre_out, u_out, v_out, ga_out, qkv_out, p_out, ctx_out, hid_out, act_out, slope_out,
    w_feat, wqkv, wout, wup, wdown, biases, boxes, w_box, key_rows,
    ga, qkv, weights, ctx, hid, act, slope, u_buf, v_buf, x_buf, load_sem, save_sem, *scratch, count
):
    group = Group(scratch[:8])
    swap = Swap(count, scratch[8:])
    me = group.me
    heads = wout_any.shape[1]
    loads, saves = Loads(load_sem), Loads(save_sem)
    feat_load = loads.start(feat_any, w_feat)
    for depth in range(LAYERS):
        clear_spare(wqkv.at[depth], wout.at[depth], heads)
    attend_loads, feed_loads = [], []
    for depth in range(LAYERS):
        attend_loads.append(
            weight_loads(loads, depth, wqkv.at[depth], wout.at[depth], (wqkv_any, wout_any))
        )
        feed_loads.append(
            [
                loads.start(wup_any.at[depth], wup.at[depth]),
                loads.start(wdown_any.at[depth], wdown.at[depth]),
            ]
        )
    greet(group.others() + swap.others())

    pad_into(boxes, boxes_ref)
    pad_into(w_box, w_box_ref)
    feat_load.wait()
    pre = dot_nn(features[...], w_feat[...])
    pre += lax.dot_general(
        boxes[...], w_box[...], (((0,), (0,)), ((), ())),
        precision=lax.Precision.HIGHEST, preferred_element_type=FULL,
    )
    pre += enc_ref[0:1]
    hat, _ = normed_rows(pre)
    swap.start((hat * as_row(gain_ref) + enc_ref[1:2]).astype(LOW))
    pre_out[...] = pre
    x_buf[0:CAP] = cap_ref[...].astype(FULL)
    place = placed(slot_ref)
    biases[...] = jnp.zeros(biases.shape, FULL)
    for depth in range(LAYERS):
        biases[depth, 0:1, 0:heads] = b_qv[depth, 0:1]
        biases[depth, 0:1, 2 * LANES : 2 * LANES + heads] = b_qv[depth, 1:2]
    spots = lax.broadcasted_iota(jnp.int32, (8, SEQ), 1)
    for image in range(GROUP):
        seen = jnp.where(
            spots < CAP, spots - caption_counts[image], spots - CAP - region_counts[image]
        )
        key_rows[image] = jnp.where(seen < 0, 0.0, -1e30)
    masks = head_masks()
    scaled = [(one.astype(FULL) * HD ** (-0.5)).astype(LOW) for one in masks]
    x_buf[CAP:] = dot_nn(place, swap.arrive().astype(LOW))

    for depth in range(LAYERS):

        def attend(image):
            rows = image_rows(image)
            low = (dot_nt(ga[depth, rows], wqkv[depth]) + biases[depth, 0:1]).astype(LOW)
            qkv[depth, rows] = low
            queries, keys_low, values_low = (
                low[:, :LANES], low[:, LANES : 2 * LANES], low[:, 2 * LANES :],
            )
            total = jnp.zeros((ROWS, LANES), FULL)
            for head in range(3):
                scores = dot_nt(queries * scaled[head], keys_low) + key_rows[image, 0:1]
                raised = jnp.exp(scores - jnp.max(scores, axis=-1, keepdims=True))
                prob = (raised * (1.0 / jnp.sum(raised, axis=-1, keepdims=True))).astype(LOW)
                weights[depth, image, head] = prob
                total += dot_nn(prob, values_low * masks[head])
            low_ctx = total.astype(LOW)
            ctx[depth, rows] = low_ctx
            return dot_nn(low_ctx, wout[depth])

        def feed(image):
            rows = image_rows(image)
            pre = dot_nn(hid[depth, rows], wup[depth]) + b_up[depth : depth + 1]
            half = 0.5 * (1.0 + lax.erf(pre * 2.0 ** (-0.5)))
            low = (pre * half).astype(LOW)
            act[depth, rows] = low
            slope[depth, rows] = (
                half + pre * jnp.exp(-0.5 * pre * pre) * 0.3989422804014327
            ).astype(LOW)
            return dot_nn(low, wdown[depth])

        states = x_buf[...]
        ga[depth, image_rows(me)] = states.astype(LOW)
        for one in attend_loads[depth]:
            one.wait()
        total = group.exchange(ga.at[depth], attend)
        for src, dst in ((ga, ga_out), (qkv, qkv_out), (weights, p_out), (ctx, ctx_out)):
            saves.start(src.at[depth], dst.at[depth])
        pre_attn = x_buf[...] + total + row_biases[depth, 0:1]
        hat, _ = normed_rows(pre_attn)
        normed = hat * norm_gains[depth, 0:1] + row_biases[depth, 1:2]
        hid[depth, image_rows(me)] = normed.astype(LOW)
        u_buf[depth] = pre_attn
        saves.start(u_buf.at[depth], u_out.at[depth])
        x_buf[...] = normed
        for one in feed_loads[depth]:
            one.wait()
        total = group.exchange(hid.at[depth], feed, late=True)
        for src, dst in ((hid, hid_out), (act, act_out), (slope, slope_out)):
            saves.start(src.at[depth], dst.at[depth])
        pre_ffn = x_buf[...] + total + row_biases[depth, 2:3]
        v_buf[depth] = pre_ffn
        saves.start(v_buf.at[depth], v_out.at[depth])
        hat, _ = normed_rows(pre_ffn)
        x_buf[...] = hat * norm_gains[depth, 1:2] + row_biases[depth, 3:4]

    x_out[...] = x_buf[...]
    swap.finish()
    for depth in range(LAYERS):
        for place, (src, dst) in enumerate(
            (
                (ga, ga_out), (qkv, qkv_out), (weights, p_out), (ctx, ctx_out), (u_buf, u_out),
                (hid, hid_out), (act, act_out), (slope, slope_out), (v_buf, v_out),
            )
        ):
            pltpu.make_async_copy(
                src.at[depth], dst.at[depth], save_sem.at[9 * depth + place]
            ).wait()


def forward(
    count, caption_counts, region_counts, features, boxes, w_box, gain, enc, captions, slots,
    b_qv, b_up, row_biases, norm_gains, w_feat, wqkv, wout, wup, wdown,
):
    width = captions.shape[1]
    hidden = wup.shape[2]
    rows = features.shape[0]
    group = GROUP * ROWS
    saved = [
        ((LAYERS, group, width), LOW),
        ((LAYERS, group, 3 * LANES), LOW),
        ((LAYERS, GROUP, 3, ROWS, ROWS), LOW),
        ((LAYERS, group, LANES), LOW),
        ((LAYERS, group, width), LOW),
        ((LAYERS, group, hidden), LOW),
        ((LAYERS, group, hidden), LOW),
    ]
    kept = ((LAYERS, ROWS, width), FULL)
    shapes = [((ROWS, width), FULL), ((rows, width), FULL), kept, kept] + saved
    vmem = pl.BlockSpec(memory_space=pltpu.VMEM)
    smem = pl.BlockSpec(memory_space=pltpu.SMEM)
    loose = pl.BlockSpec(memory_space=pl.ANY)
    return pl.pallas_call(
        functools.partial(forward_kernel, count=count),
        out_shape=[jax.ShapeDtypeStruct(*one) for one in shapes],
        in_specs=[smem] * 2 + [vmem] * 11 + [loose] * 5,
        out_specs=[vmem] * 2 + [loose] * 9,
        scratch_shapes=[
            pltpu.VMEM(w_feat.shape, LOW),
            pltpu.VMEM((LAYERS, 3 * LANES, width), LOW),
            pltpu.VMEM((LAYERS, LANES, width), LOW),
            pltpu.VMEM(wup.shape, LOW),
            pltpu.VMEM(wdown.shape, LOW),
            pltpu.VMEM((LAYERS, 8, 3 * LANES), FULL),
            pltpu.VMEM((8, rows), FULL),
            pltpu.VMEM((8, width), FULL),
            pltpu.VMEM((GROUP, 8, SEQ), FULL),
        ]
        + [pltpu.VMEM(*one) for one in saved]
        + [pltpu.VMEM(*kept), pltpu.VMEM(*kept), pltpu.VMEM((ROWS, width), FULL)]
        + [pltpu.SemaphoreType.DMA((1 + 6 * LAYERS,)), pltpu.SemaphoreType.DMA((9 * LAYERS,))]
        + group_scratch(width)
        + swap_scratch(rows, width, count),
        compiler_params=pltpu.CompilerParams(
            collective_id=0, has_side_effects=True, vmem_limit_bytes=60 * 2**20
        ),
    )(
        caption_counts, region_counts, features, boxes, w_box, gain, enc, captions, slots,
        b_qv, b_up, row_biases, norm_gains, w_feat, wqkv, wout, wup, wdown,
    )


def ring_places(count):
    me = lax.axis_index("dp")
    half = count // 2

    def device(place):
        side = place // half
        depth = place + side * (count - 1 - 2 * place)
        return 2 * depth + side

    side = lax.rem(me, 2)
    depth = me // 2
    place = depth + side * (count - 1 - 2 * depth)
    return place, device(lax.rem(place + 1, count)), device(lax.rem(place + count - 1, count))


def ring_rows(length, count):
    each = -(-length // (16 * count))
    first = 16 * (each // 2)
    sizes = (first, 16 * each - first) if first else (16 * each,)
    return count * each * 16, sizes


class Ring:
    def __init__(self, count, places, pack, lands, sems, passed=None, flush=None):
        self.count, self.last = count, count - 1
        self.place, self.after, self.before = places
        self.pack, self.lands, self.sems = pack, lands, sems
        self.sizes = [land.shape[1] for land in lands]
        self.ways = range(len(self.sizes))
        self.taken, self.due = 0, 0
        self.passed, self.flush, self.prepare = passed, flush, None

    def chunk(self, way, offset):
        spot = lax.rem(self.place + (offset if way else -offset) + 2 * self.count, self.count)
        start = spot * sum(self.sizes) + way * self.sizes[0]
        return pl.ds(pl.multiple_of(start, 16), self.sizes[way])

    def copy(self, phase, way, step, rows=None):
        if phase == 0:
            src = self.pack.at[self.chunk(way, 0)] if step == 0 else self.lands[way].at[step - 1]
            dst = self.lands[way].at[step]
        else:
            if rows is None:
                rows = self.chunk(way, step - 1)
            src = self.pack.at[rows]
            dst = self.pack.at[rows]
        return remote(
            src, dst, self.sems.at[2 * phase, way, step], self.sems.at[2 * phase + 1, way, step],
            {"dp": self.before if way else self.after},
        )

    def running(self):
        return self.taken <= 2 * self.last

    def step(self):
        index, last = self.taken, self.last
        if self.prepare is not None and index <= last:
            self.prepare(index)
        for way in self.ways:
            if index == 0:
                self.copy(0, way, 0).start()
            elif index <= last:
                done = index - 1
                self.copy(0, way, done).wait_recv()
                if done == 0:
                    self.copy(0, way, 0).wait_send()
                rows = self.chunk(way, done + 1)
                added = (self.lands[way][done].astype(FULL) + self.pack[rows].astype(FULL)).astype(LOW)
                if index < last:
                    self.lands[way][done] = added
                    self.copy(0, way, index).start()
                else:
                    self.pack[rows] = added
                    self.copy(1, way, 0).start()
                    self.pass_on(rows)
            else:
                done = index - last - 1
                rows = self.chunk(way, done)
                self.copy(1, way, done, rows).wait_recv()
                if done + 1 < last:
                    self.copy(1, way, done + 1).start()
                self.pass_on(rows)
        self.taken += 1
        if not self.running() and self.flush is not None:
            self.flush()

    def pass_on(self, rows):
        if self.passed is not None:
            self.passed(rows)

    def finish(self):
        for phase in range(2):
            for way in self.ways:
                for step in range(1 - phase, self.last):
                    self.copy(phase, way, step).wait_send()


class Clock:
    def __init__(self):
        self.now, self.link, self.rings = 0, 0, []

    def add(self, ring):
        ring.due = self.now
        self.rings.append(ring)

    def running(self):
        return [ring for ring in self.rings if ring.running()]

    def visit(self, ring):
        self.now = max(self.now, ring.due)
        ring.step()
        self.link = max(self.link, self.now) + max(ring.sizes) * 0.036
        ring.due = self.link + 2

    def tick(self, weight):
        self.now += weight
        for ring in sorted(self.running(), key=lambda one: one.due):
            if ring.due <= self.now:
                self.visit(ring)

    def drain(self, first):
        while self.running():
            self.visit(
                min(
                    self.running(),
                    key=lambda one: one.due + 1.5 * one.taken - (3 if one is first else 0),
                )
            )


def backward_kernel(
    cot_ref, slot_ref, boxes_ref, gain_ref, pre_ref, norm_gains,
    wqkv_any, wout_any, wup_any, wdown_any, u_any, v_any,
    ga_any, qkv_any, p_any, ctx_any, hid_any, act_any, slope_any, feat_any, w_feat_any,
    cap_out, back_out, box_out, gain_out, enc_out, qv_out, up_sum_out, norms_out, rows_out,
    down_out, up_out, out_out, mixed_out, feat_out,
    wqkv, wout, wup, wdown, u_buf, v_buf,
    ga, qkv, weights, ctx, hid, act, slope, low_e, d_up, low_f, d_mixed,
    keep, small, small_in, extra_sum, extra_in, down_pack, up_pack, thin_pack, ring_sems,
    features, boxes, feat_in, feat_send, feat_pack, feat_sems, cross_sems,
    send, recv, small_send, small_recv, load_sem, local_sem, *scratch, count, ways
):
    group = Group(scratch[:8])
    swap = Swap(count, scratch[8:13])
    lands = list(scratch[13:])
    down_lands, up_lands, thin_lands, feat_lands = (
        [lands.pop(0) for _ in range(number)] for number in ways
    )
    me, mate, peer, diag = group.me, group.mate, group.peer, group.diag
    width = keep.shape[1]
    heads = wout_any.shape[1]
    hidden = act.shape[1]
    loads, local = Loads(load_sem), Loads(local_sem)

    def feed_load(depth):
        return [
            loads.start(src.at[depth], dst)
            for src, dst in (
                (v_any, v_buf), (wdown_any, wdown), (slope_any, slope), (wup_any, wup),
                (act_any, act), (hid_any, hid),
            )
        ]

    def attend_load(depth):
        return [
            loads.start(src.at[depth], dst)
            for src, dst in (
                (u_any, u_buf), (p_any, weights), (qkv_any, qkv), (ctx_any, ctx), (ga_any, ga),
            )
        ] + weight_loads(loads, depth, wqkv, wout, (wqkv_any, wout_any))

    feed_waits = feed_load(LAYERS - 1)
    clear_spare(wqkv, wout, heads)
    attend_waits = attend_load(LAYERS - 1)
    greet(group.others() + swap.others())
    places = ring_places(count)

    def down_flush(depth):
        local.start(down_pack.at[depth, pl.ds(0, hidden)], down_out.at[depth])

    def up_flush(depth):
        local.start(up_pack.at[depth, pl.ds(0, width)], up_out.at[depth])

    def thin_flush(depth):
        local.start(thin_pack.at[depth, pl.ds(0, heads)], out_out.at[depth])
        for kind in range(3):
            rows = pl.ds(heads * (kind + 1), heads)
            local.start(thin_pack.at[depth, rows], mixed_out.at[depth, kind])

    def rings(spot, pack, own_lands, flush):
        return [
            Ring(
                count, places, pack.at[depth], [one.at[depth] for one in own_lands],
                ring_sems.at[spot, depth], flush=functools.partial(flush, depth),
            )
            for depth in range(LAYERS)
        ]

    downs = rings(0, down_pack, down_lands, down_flush)
    ups = rings(1, up_pack, up_lands, up_flush)
    thins = rings(2, thin_pack, thin_lands, thin_flush)
    clock = Clock()
    tick = clock.tick
    masks = head_masks()

    for depth in reversed(range(LAYERS)):

        def feed_back(image):
            rows = image_rows(image)
            low = (dot_nt(low_e[rows], wdown[...]) * slope[rows].astype(FULL)).astype(LOW)
            d_up[rows] = low
            tick(0.8)
            return dot_nt(low, wup[...])

        def attend_back(image):
            rows = image_rows(image)
            d_ctx = dot_nt(low_f[rows], wout[...]).astype(LOW)
            low = qkv[rows]
            queries, keys_low, values_low = (
                low[:, :LANES], low[:, LANES : 2 * LANES], low[:, 2 * LANES :],
            )
            d_q = jnp.zeros((ROWS, LANES), FULL)
            d_k = jnp.zeros((ROWS, LANES), FULL)
            d_v = jnp.zeros((ROWS, LANES), FULL)
            for head in range(3):
                own = d_ctx * masks[head]
                prob_low = weights[image, head]
                d_v += dot_tn(prob_low, own)
                d_prob = dot_nt(own, values_low)
                prob = prob_low.astype(FULL)
                meant = jnp.sum(prob * d_prob, axis=-1, keepdims=True)
                d_score = (prob * (d_prob - meant)).astype(LOW)
                d_q += dot_nn(d_score, keys_low * masks[head])
                d_k += dot_tn(d_score, queries * masks[head])
                tick(1.2)
            scaling = HD ** (-0.5)
            d_mixed[rows, 0:LANES] = (d_q * scaling).astype(LOW)
            d_mixed[rows, LANES : 2 * LANES] = (d_k * scaling).astype(LOW)
            d_mixed[rows, 2 * LANES : 3 * LANES] = d_v.astype(LOW)
            return dot_nn(d_mixed[rows], wqkv[...])

        def down_fill(start):
            def fill():
                down_pack[depth, start : start + LANES] = dot_tn(
                    act[:, start : start + LANES], low_e[...]
                ).astype(LOW)

            return fill

        def up_fill(start):
            def fill():
                up_pack[depth, start : start + LANES] = dot_tn(
                    hid[:, start : start + LANES], d_up[...]
                ).astype(LOW)

            return fill

        def out_fill():
            thin_pack[depth, 0:heads] = dot_tn(ctx[...], low_f[...])[:heads].astype(LOW)

        def mixed_fill(kind):
            def fill():
                base = heads * (kind + 1)
                made = dot_tn(d_mixed[:, kind * LANES : (kind + 1) * LANES], ga[...])
                thin_pack[depth, base : base + heads] = made[:heads].astype(LOW)

            return fill

        def small_copy(spot, target):
            return remote(
                small.at[depth], small_in.at[depth, spot],
                small_send.at[depth, spot], small_recv.at[depth, spot], {"mp": target},
            )

        first, second = small_copy(0, mate), small_copy(1, peer)

        def small_fill():
            first.wait_recv()
            first.wait_send()
            small[depth] += small_in[depth, 0]
            second.start()

        gradient = cot_ref[...].astype(FULL) if depth == LAYERS - 1 else keep[...]
        feed_waits[0].wait()
        d_pre, hat = normed_back(gradient, v_buf[...], norm_gains[depth, 1:2])
        low_e[image_rows(me)] = d_pre.astype(LOW)
        keep[...] = d_pre
        small[depth] = jnp.zeros((8, width), FULL)
        small[depth, 1:2] = row_sum(gradient * hat)
        small[depth, 4:5] = row_sum(d_pre)
        small[depth, 5:6] = row_sum(gradient)
        for one in feed_waits[1:]:
            one.wait()
        total = group.exchange(
            low_e, feed_back, tick,
            [down_fill(start) for start in range(0, hidden, LANES)]
            + [functools.partial(clock.add, downs[depth])]
            + [up_fill(start) for start in range(0, width, LANES)]
            + [functools.partial(clock.add, ups[depth])],
        )
        tick(2)
        b_up_sum = row_sum(d_up[...].astype(FULL))
        if depth:
            feed_waits = feed_load(depth - 1)
        gradient = keep[...] + total
        if depth < LAYERS - 1:
            pass
        attend_waits[0].wait()
        d_pre, hat = normed_back(gradient, u_buf[...], norm_gains[depth, 0:1])
        low_f[image_rows(me)] = d_pre.astype(LOW)
        keep[...] = d_pre
        small[depth, 0:1] = row_sum(gradient * hat)
        small[depth, 2:3] = row_sum(d_pre)
        small[depth, 3:4] = row_sum(gradient)
        first.start()
        for one in attend_waits[1:]:
            one.wait()
        total = group.exchange(
            low_f, attend_back, tick,
            [small_fill, out_fill]
            + [mixed_fill(kind) for kind in range(3)]
            + [functools.partial(clock.add, thins[depth])],
            late=True,
        )
        tick(2)
        second.wait_recv()
        second.wait_send()
        small[depth] += small_in[depth, 1]
        small[depth, 6:7] = b_up_sum
        small[depth, 7:8] = row_sum(d_mixed[...].astype(FULL))
        if depth:
            attend_waits = attend_load(depth - 1)
        keep[...] += total

    cap_out[...] = keep[0:CAP]
    place = placed(slot_ref)
    swap.start(dot_tn(place, keep[CAP:].astype(LOW)).astype(LOW))
    span = act.shape[0]
    feat_loads = [
        loads.start(feat_any, features),
        loads.start(w_feat_any.at[pl.ds(0, span)], act),
        loads.start(w_feat_any.at[pl.ds(span, span)], slope),
    ]
    pad_into(boxes, boxes_ref)
    each = feat_send.shape[0]
    gradient = swap.arrive()
    tick(6)
    d_pre, hat = normed_back(gradient, pre_ref[...], as_row(gain_ref))
    low = d_pre.astype(LOW)
    feat_loads[0].wait()

    def product(ref, spot):
        columns = pl.ds(pl.multiple_of(spot * each, 128), each)
        ref[0:each] = dot_tn(features[:, columns], low).astype(LOW)

    def copy(src, dst, spot, target):
        return remote(src, dst, send.at[spot], recv.at[spot], {"mp": target})

    span_rows = pl.ds(0, each)
    to_mate = [
        copy(low_e.at[span_rows], feat_in.at[0], 0, mate),
        copy(d_up.at[span_rows], feat_in.at[1], 1, mate),
    ]
    product(low_e, diag)
    to_mate[0].start()
    product(low_f, peer)
    tick(1.5)
    to_mate[0].wait_recv()
    feat_send[...] = (low_f[0:each].astype(FULL) + feat_in[0].astype(FULL)).astype(LOW)
    feat = Ring(count, places, feat_pack, feat_lands, feat_sems)

    def crossing(way, step):
        rows = feat.chunk(way, step)
        return rows, remote(
            feat_send.at[rows], feat_in.at[2, rows],
            cross_sems.at[0, way, step], cross_sems.at[1, way, step], {"mp": peer},
        )

    def crossings(action):
        for step in range(count):
            for way in feat.ways:
                rows, one = crossing(way, step)
                pl.when(rows.start < each)(functools.partial(action, one))

    def added(step):
        for way in feat.ways:
            rows, one = crossing(way, step)

            @pl.when(rows.start < each)
            def _():
                one.wait_recv()
                feat_pack[rows] = (hid[rows].astype(FULL) + feat_in[2, rows].astype(FULL)).astype(LOW)

    feat.prepare = added
    crossings(lambda one: one.start())
    tick(2)
    rounded = low.astype(FULL)
    extra_sum[...] = jnp.concatenate(
        [
            lax.dot_general(
                boxes[...], rounded, (((1,), (0,)), ((), ())),
                precision=lax.Precision.HIGHEST, preferred_element_type=FULL,
            ),
            row_sum(gradient * hat),
            row_sum(rounded),
            row_sum(gradient),
            jnp.zeros((5, width), FULL),
        ],
        axis=0,
    )
    extras = [copy(extra_sum, extra_in.at[spot], 6 + spot, target) for spot, target in ((0, mate), (1, peer))]
    extras[0].start()
    product(d_up, mate)
    to_mate[1].start()
    tick(1)
    product(hid, me)
    tick(1)
    extras[0].wait_recv()
    extras[0].wait_send()
    extra_sum[...] += extra_in[0]
    extras[1].start()
    feat_loads[1].wait()
    back_out[:, 0:span] = dot_nt(low, act[...])
    tick(1)
    feat_loads[2].wait()
    back_out[:, span:] = dot_nt(low, slope[...])
    to_mate[1].wait_recv()
    own = hid[0:each].astype(FULL) + feat_in[1].astype(FULL)
    hid[0:each] = own.astype(LOW)
    tick(1.5)
    extras[1].wait_recv()
    extras[1].wait_send()
    base = each + 16
    feat_pack[each:base] = (extra_sum[...] + extra_in[1]).astype(LOW)
    for depth in range(LAYERS):
        feat_pack[base : base + 16] = jnp.concatenate(
            [small[depth], jnp.zeros((8, width), FULL)], axis=0
        ).astype(LOW)
        base += 16
    feat_rows = feat_pack.shape[0]
    if feat_rows > base:
        feat_pack[base:] = jnp.zeros((feat_rows - base, width), LOW)
    def ours(spot, start, size):
        return feat_out.at[pl.ds(pl.multiple_of(spot * each + start, 16), size)]

    def spread(rows):
        @pl.when(rows.start < each)
        def _():
            for spot, target in ((3, peer), (4, mate)):
                copy(feat_pack.at[rows], ours(me, rows.start, rows.size), spot, target).start()

    feat.passed = spread
    clock.add(feat)
    clock.drain(feat)
    local.start(feat_pack.at[span_rows], ours(me, 0, each))
    base = each
    box_out[...] = feat_pack[base : base + 16].astype(FULL)[0:4]
    gain_out[...] = feat_pack[base : base + 16].astype(FULL)[8:9]
    enc_out[...] = feat_pack[base : base + 16].astype(FULL)[9:11]
    for depth in range(LAYERS):
        base += 16
        sums = feat_pack[base : base + 16].astype(FULL)
        norms_out[depth] = sums[0:2]
        rows_out[depth] = sums[2:6]
        up_sum_out[depth : depth + 1] = sums[6:7]
        qv_out[depth, 0:1] = sums[7:8, 0:heads]
        qv_out[depth, 1:2] = sums[7:8, 2 * LANES : 2 * LANES + heads]
    copy(feat_send, ours(peer, 0, each), 3, peer).wait_recv()
    relay = copy(ours(peer, 0, each), ours(peer, 0, each), 5, mate)
    relay.start()
    copy(feat_send, ours(mate, 0, each), 4, mate).wait_recv()
    copy(feat_send, ours(diag, 0, each), 5, mate).wait_recv()
    for spot in (3, 4):
        copy(feat_send, ours(me, 0, each), spot, mate).wait_send()
    for one in to_mate + [relay]:
        one.wait_send()
    crossings(lambda one: one.wait_send())
    for ring in downs + ups + thins + [feat]:
        ring.finish()
    swap.finish()
    for one in local.made:
        one.wait()


def backward(
    count, cotangent, slots, boxes, gain, pre, norm_gains, wqkv, wout, wup, wdown, kept,
    features, w_feat,
):
    width = cotangent.shape[1]
    rows, columns = features.shape
    hidden = wup.shape[2]
    heads = wout.shape[1]
    group = GROUP * ROWS
    each = columns // GROUP
    down_rows, down_sizes = ring_rows(hidden, count)
    up_rows, up_sizes = ring_rows(width, count)
    thin_rows, thin_sizes = ring_rows(GROUP * heads, count)
    feat_rows, feat_sizes = ring_rows(each + 16 + 16 * LAYERS, count)

    ways = max(len(one) for one in (down_sizes, up_sizes, thin_sizes, feat_sizes))

    def ring_sems(*lead):
        return pltpu.SemaphoreType.DMA(lead + (4, ways, count - 1))

    vmem = pl.BlockSpec(memory_space=pltpu.VMEM)
    loose = pl.BlockSpec(memory_space=pl.ANY)
    packs = [((LAYERS, size, width), LOW) for size in (down_rows, up_rows, thin_rows)]
    shapes = [
        ((CAP, width), FULL),
        ((rows, columns), FULL),
        ((4, width), FULL),
        ((1, width), FULL),
        ((2, width), FULL),
        ((LAYERS, 2, heads), FULL),
        ((LAYERS, hidden), FULL),
        ((LAYERS, 2, width), FULL),
        ((LAYERS, 4, width), FULL),
        ((LAYERS, hidden, width), LOW),
        ((LAYERS, width, hidden), LOW),
        ((LAYERS, heads, width), LOW),
        ((LAYERS, 3, heads, width), LOW),
        ((columns, width), LOW),
    ]
    return pl.pallas_call(
        functools.partial(
            backward_kernel,
            count=count,
            ways=[len(one) for one in (down_sizes, up_sizes, thin_sizes, feat_sizes)],
        ),
        out_shape=[jax.ShapeDtypeStruct(*one) for one in shapes],
        in_specs=[vmem] * 6 + [loose] * 15,
        out_specs=[vmem] * 9 + [loose] * 5,
        scratch_shapes=[
            pltpu.VMEM((3 * LANES, width), LOW),
            pltpu.VMEM((LANES, width), LOW),
            pltpu.VMEM(wup.shape[1:], LOW),
            pltpu.VMEM(wdown.shape[1:], LOW),
            pltpu.VMEM((ROWS, width), FULL),
            pltpu.VMEM((ROWS, width), FULL),
        ]
        + [pltpu.VMEM(one.shape[1:], one.dtype) for one in kept[2:]]
        + [
            pltpu.VMEM((group, width), LOW),
            pltpu.VMEM((group, hidden), LOW),
            pltpu.VMEM((group, width), LOW),
            pltpu.VMEM((group, 3 * LANES), LOW),
            pltpu.VMEM((ROWS, width), FULL),
            pltpu.VMEM((LAYERS, 8, width), FULL),
            pltpu.VMEM((LAYERS, 2, 8, width), FULL),
            pltpu.VMEM((16, width), FULL),
            pltpu.VMEM((2, 16, width), FULL),
        ]
        + [pltpu.VMEM(*one) for one in packs]
        + [ring_sems(3, LAYERS)]
        + [
            pltpu.VMEM(features.shape, LOW),
            pltpu.VMEM((8, rows), FULL),
            pltpu.VMEM((3, each, width), LOW),
            pltpu.VMEM((each, width), LOW),
            pltpu.VMEM((feat_rows, width), LOW),
            ring_sems(),
            pltpu.SemaphoreType.DMA((2, ways, count)),
            pltpu.SemaphoreType.DMA((8,)),
            pltpu.SemaphoreType.DMA((8,)),
            pltpu.SemaphoreType.DMA((LAYERS, 2)),
            pltpu.SemaphoreType.DMA((LAYERS, 2)),
            pltpu.SemaphoreType.DMA((15 * LAYERS + 3,)),
            pltpu.SemaphoreType.DMA((1 + 6 * LAYERS,)),
        ]
        + group_scratch(width)
        + swap_scratch(rows, width, count)
        + [
            pltpu.VMEM((LAYERS, count - 1, size, width), LOW) for size in down_sizes + up_sizes + thin_sizes
        ]
        + [pltpu.VMEM((count - 1, size, width), LOW) for size in feat_sizes],
        compiler_params=pltpu.CompilerParams(
            collective_id=1, has_side_effects=True, vmem_limit_bytes=62 * 2**20
        ),
    )(
        cotangent, slots, boxes, gain, pre, norm_gains, wqkv, wout, wup, wdown, *kept,
        features, w_feat,
    )


def finish_kernel(*refs):
    half = len(refs) // 2
    for src, dst in zip(refs[:half], refs[half:]):
        values = src[...].astype(FULL)
        dst[...] = values.reshape(dst.shape) if len(dst.shape) == 1 else values


def finish(tall, small, shapes):
    blocks = 8
    tall = [one.reshape(-1, one.shape[-1]) for one in tall]
    specs = [
        pl.BlockSpec((one.shape[0] // blocks, one.shape[1]), lambda step: (step, 0)) for one in tall
    ]
    whole = [pl.BlockSpec(memory_space=pltpu.VMEM)] * len(small)
    made = pl.pallas_call(
        finish_kernel,
        grid=(blocks,),
        out_shape=[jax.ShapeDtypeStruct(one.shape, FULL) for one in tall]
        + [jax.ShapeDtypeStruct(one, FULL) for one in shapes],
        in_specs=specs + whole,
        out_specs=specs + whole,
        compiler_params=pltpu.CompilerParams(vmem_limit_bytes=62 * 2**20),
    )(*tall, *small)
    return made[: len(tall)], made[len(tall) :]


def on_device(
    captions,
    features,
    region_boxes,
    caption_counts,
    region_counts,
    slot_map,
    w_feat,
    w_box,
    enc_gain,
    enc_vectors,
    w_qkv,
    b_qv,
    w_out,
    w_up,
    b_up,
    w_down,
    norm_gains,
    row_biases,
    cotangent,
):
    count = lax.axis_size("dp")
    wqkv = w_qkv.transpose(0, 2, 3, 1)
    layer_output, enc_pre, *kept = forward(
        count, caption_counts, region_counts, features, region_boxes, w_box, enc_gain, enc_vectors,
        captions, slot_map, b_qv, b_up, row_biases, norm_gains, w_feat, wqkv, w_out, w_up, w_down,
    )
    (
        caption_grad, feature_grad, box_sum, gain_sum, enc_sum, qv_sum, up_sum, norm_sum, row_sums,
        down, up, out, mixed, feat,
    ) = backward(
        count, cotangent, slot_map, region_boxes, enc_gain, enc_pre, norm_gains, wqkv, w_out, w_up,
        w_down, kept, features, w_feat,
    )
    tall, sums = finish(
        [layer_output, caption_grad, feature_grad, feat, mixed, out, up, down],
        [box_sum, gain_sum, enc_sum, qv_sum, up_sum, norm_sum, row_sums],
        [box_sum.shape, enc_gain.shape] + [one.shape for one in (enc_sum, qv_sum, up_sum, norm_sum, row_sums)],
    )
    layer_output, caption_grad, feature_grad, feat, mixed_grad, out_grad, up_grad, down_grad = tall
    box_sum, gain_sum, enc_sum, qv_sum, up_sum, norm_sum, row_sums = sums
    return (
        layer_output,
        caption_grad,
        feature_grad,
        feat,
        box_sum,
        gain_sum,
        enc_sum,
        mixed_grad.reshape(mixed.shape).transpose(0, 3, 1, 2),
        qv_sum,
        out_grad.reshape(out.shape),
        up_grad.reshape(up.shape),
        up_sum,
        down_grad.reshape(down.shape),
        norm_sum,
        row_sums,
    )


def solution(mesh):
    return jax.shard_map(
        on_device,
        mesh=mesh,
        in_specs=(
            P(("dp", "mp"), None),
            P(("dp", "mp"), None),
            P(None, ("dp", "mp")),
            P("dp"),
            P("dp"),
            P(("dp", "mp"), None),
            P(),
            P(),
            P(),
            P(),
            P(None, None, None, "mp"),
            P(None, None, "mp"),
            P(None, "mp", None),
            P(None, None, "mp"),
            P(None, "mp"),
            P(None, "mp", None),
            P(),
            P(),
            P(("dp", "mp"), None),
        ),
        out_specs=(
            P(("dp", "mp"), None),
            P(("dp", "mp"), None),
            P(("dp", "mp"), None),
            P(),
            P(),
            P(),
            P(),
            P(None, None, None, "mp"),
            P(None, None, "mp"),
            P(None, "mp", None),
            P(None, None, "mp"),
            P(None, "mp"),
            P(None, "mp", None),
            P(),
            P(),
        ),
        check_vma=False,
    )
```
